32 devices in a mesh: parts: 2 (over y), grp: 4 (over x, core), ep: 4 (over z).
Axes of the slice: x: 2, y: 2, z: 4, core: 2. Of those that a mesh axis runs over, the one named last changes fastest.
Arguments:
- tokens: bfloat16 [4096, 1024], P(('parts', 'grp', 'ep')), parts along dimension 0, may hold values from -6 to 6
- cotangent: bfloat16 [4096, 1024], P(('parts', 'grp', 'ep')), parts along dimension 0, may hold values from -6 to 6
- expert_ids: int32 [4096, 5], P(('parts', 'grp', 'ep')), parts along dimension 0, may hold values from 0 to 15, all different within a row; in each aligned block of 128 rows (0 to 127, 128 to 255, ...) at most 80 rows name the same one
- route_weights: float32 [4096, 5], P(('parts', 'grp', 'ep')), parts along dimension 0, may hold values from 0.1 to 1
- w_gate: bfloat16 [16, 1024, 512], P(('grp', 'ep')), may hold values from -0.1875 to 0.1875
- w_up: bfloat16 [16, 1024, 512], P(('grp', 'ep')), may hold values from -0.1875 to 0.1875
- w_down: bfloat16 [16, 512, 1024], P(('grp', 'ep')), may hold values from -0.25 to 0.25
Outputs:
- grad_tokens: bfloat16 [4096, 1024], P(('parts', 'grp', 'ep')), parts along dimension 0
- grad_weights: bfloat16 [4096, 5], P(('parts', 'grp', 'ep')), parts along dimension 0
The draws below stay inside these ranges and needn't reach their ends.
There are 2 independent parts, one for each index of `parts`. The reference program is written for one: setup_inputs(seed, part) draws one part's arguments, and reference() takes and returns one part's arrays. A program takes and returns all parts, laid end to end along the dimension named above; an argument that names none is the same for every part. Nothing has to cross between parts.
Inputs may be any that keep to these rules, and one draw needn't show every extreme that they name: `expert_ids`: each row names 5 different experts. In each aligned block of 128 rows (the rows of one device) no expert is named by more than 80 rows, a bound that some block reaches.
All inputs are finite; a program needn't handle non-finite values.
Results may differ from the reference program's by a relative error of at most 0.0057.
Values may be sent and summed in bfloat16 or wider, within the bound.
No kernel may reach another device: no remote copies, remote signals or barrier semaphores. Data moves between devices by JAX's collectives and lax.ppermute only.
A program may use at most 64 MiB of HBM per device.

```python
import math
import jax
import jax.numpy as jnp
import numpy as np
from jax import lax

D = 1024
FF = 512
TOPK = 5
TOK_DEV = 128
EXPERTS = 16
CAP = 80
TOKENS = 2048
N_GRP = 4
N_EP = 4


def block_levels(rng, extent, split, least, largest):
    def one(axis_at, parts):
        steps = jax.random.uniform(jax.random.fold_in(jax.random.fold_in(rng, 6), axis_at), (parts,), jnp.float32, least / len(split), largest / len(split))
        return jnp.repeat(jnp.exp(steps), extent[axis_at] // parts).reshape((-1,) + (1,) * (len(extent) - axis_at - 1))

    factor_of = one(*split[0])
    for cut in split[1:]:
        factor_of = factor_of * one(*cut)
    return factor_of


def assign_block(rng, own, number, rows, amount, top, limit, slope):
    ranking = jax.random.permutation(rng, amount)
    crowded, ordinary = load_shares(amount, rows * top, limit, slope, True), load_shares(amount, rows * top, limit, slope, False)
    places = jnp.arange(amount)

    def named(sizes, turn):
        used = int((sizes > 0).sum())
        fixed = max(1, used // 4)
        shifted = fixed + (places - fixed + turn * (used - fixed)) % max(1, amount - fixed)
        return jnp.zeros((amount,), jnp.int32).at[ranking[jnp.where(places < fixed, places, shifted)]].set(jnp.asarray(sizes, jnp.int32))

    sizes = jnp.where(number % 4 == 0, named(crowded, number // 4), named(ordinary, number - number // 4 - 1))
    mixed = jax.random.permutation(jax.random.fold_in(own, 3), amount)
    source_of, taker = mixed[0:amount // 2 * 2:2], mixed[1:amount // 2 * 2:2]
    slack = jnp.minimum(sizes[source_of] - 1, limit - sizes[taker]) // 2
    slack = jnp.where((source_of == ranking[0]) | (taker == ranking[0]) | (sizes[taker] == 0), 0, jnp.maximum(slack, 0))
    shifted = jax.random.randint(jax.random.fold_in(own, 4), (amount // 2,), 0, 1 << 20) % (slack + 1)
    sizes = sizes.at[source_of].add(-shifted).at[taker].add(shifted)
    items = jnp.searchsorted(jnp.cumsum(sizes), jnp.arange(rows * top), side="right").astype(jnp.int32)
    grid = items.reshape(top, rows).T
    grid = grid[jax.random.permutation(jax.random.fold_in(own, 1), rows)]
    turn = jax.random.randint(jax.random.fold_in(own, 2), (rows, 1), 0, top)
    return jnp.take_along_axis(grid, (jnp.arange(top)[None, :] + turn) % top, axis=1)


def load_shares(count, total, most, skew, full):
    weights = [(1 << 20) // math.isqrt(standing ** skew) + 1 for standing in range(1, count + 1)]
    largest = most if full else min(most, max(-(-total // count), total * weights[0] // sum(weights)))
    least = 1 if total - largest >= count - 1 else 0
    holding, spare = [largest] + [least] * (count - 1), total - largest - least * (count - 1)
    while spare > 0:
        movable = [i for i in range(1, count) if holding[i] < largest] or [i for i in range(1, count) if holding[i] < most]
        whole, budget = sum([weights[i] for i in movable]), spare
        for i in movable:
            more = min(most - holding[i], max(1, budget * weights[i] // whole), spare)
            holding[i] = holding[i] + more
            spare = spare - more
    return np.array(holding)


def gaussian(rng, dims, scale, most, split=(), kind=jnp.bfloat16):
    values = scale * jax.random.normal(rng, dims, jnp.float32)
    if split:
        values = values * block_levels(rng, dims, split, -0.22, 0.18)
    return jnp.clip(values, -most, most).astype(kind)


def setup_inputs(seed: int = 0, part: int = 0) -> dict:
    key_of = jax.random.split(jax.random.key(seed), 8)
    part_splits = jax.random.split(jax.random.fold_in(key_of[7], part), 8)
    tokens = gaussian(part_splits[0], (TOKENS, D), 1.0, 6.0, ((0, 16),))
    cotangent = gaussian(part_splits[1], (TOKENS, D), 1.0, 6.0, ((0, 16),))
    expert_ids_keys = jax.random.split(jax.random.fold_in(part_splits[2], 1), TOKENS // TOK_DEV)
    expert_ids_turns = jax.random.permutation(jax.random.fold_in(part_splits[2], 3), TOKENS // TOK_DEV)
    expert_ids = jax.vmap(lambda own, number: assign_block(jax.random.fold_in(part_splits[2], 2), own, number, TOK_DEV, EXPERTS, TOPK, CAP, 2))(expert_ids_keys, expert_ids_turns).reshape((TOKENS, TOPK))
    route_weights = jnp.clip(jnp.exp(math.log(1.0) - 2.3025851 * jax.random.uniform(part_splits[3], (TOKENS, TOPK), jnp.float32) ** block_levels(part_splits[3], (TOKENS, TOPK), ((0, 16),), -0.2, 0.2)), 0.1, 1.0)
    w_gate = gaussian(key_of[4], (EXPERTS, D, FF), D ** -0.5, 0.1875, ((0, 16),))
    w_up = gaussian(key_of[5], (EXPERTS, D, FF), D ** -0.5, 0.1875, ((0, 16),))
    w_down = gaussian(key_of[6], (EXPERTS, FF, D), FF ** -0.5, 0.25, ((0, 16),))
    return {"tokens": tokens, "cotangent": cotangent, "expert_ids": expert_ids, "route_weights": route_weights, "w_gate": w_gate, "w_up": w_up, "w_down": w_down}


def expert_grads(rows_in, grads_in, w_gate, w_up, w_down):
    contract = (((1,), (1,)), ((), ()))
    gate_pre = jnp.dot(rows_in, w_gate, preferred_element_type=jnp.float32)
    up_pre = jnp.dot(rows_in, w_up, preferred_element_type=jnp.float32)
    hidden_grad = lax.dot_general(grads_in, w_down, contract, preferred_element_type=jnp.float32)
    sigmoid_gate = jax.nn.sigmoid(gate_pre)
    activation = gate_pre * sigmoid_gate
    hidden = activation * up_pre
    weight_grad = jnp.sum(hidden_grad * hidden, axis=-1).astype(jnp.bfloat16)
    grad_up = (hidden_grad * activation).astype(jnp.bfloat16)
    grad_gate = (hidden_grad * up_pre * sigmoid_gate * (1.0 + gate_pre * (1.0 - sigmoid_gate))).astype(jnp.bfloat16)
    row_terms = (lax.dot_general(grad_gate, w_gate, contract, preferred_element_type=jnp.float32)
                 + lax.dot_general(grad_up, w_up, contract, preferred_element_type=jnp.float32)).astype(jnp.bfloat16)
    return row_terms, weight_grad


def reference(tokens, cotangent, expert_ids, route_weights, w_gate, w_up, w_down):
    token_count, top_count = expert_ids.shape
    model_width = tokens.shape[1]
    experts = w_gate.shape[0]
    expert_slots = N_GRP * N_EP * CAP
    flat_ids = expert_ids.reshape(-1).astype(jnp.int32)
    pair_count = flat_ids.shape[0]
    sort_order = jnp.argsort(flat_ids, stable=True).astype(jnp.int32)
    counts = jnp.zeros((experts,), jnp.int32).at[flat_ids].add(1)
    starts = jnp.cumsum(counts) - counts
    sorted_ids = flat_ids[sort_order]
    slot_rank = (jnp.arange(pair_count, dtype=jnp.int32) - starts[sorted_ids]).astype(jnp.int32)
    slot_table = jnp.full((experts, expert_slots), pair_count, jnp.int32).at[sorted_ids, slot_rank].set(sort_order)
    token_pad = jnp.concatenate([tokens, jnp.zeros((1, model_width), tokens.dtype)], 0)
    grad_pad = jnp.concatenate([cotangent, jnp.zeros((1, model_width), cotangent.dtype)], 0)
    weight_pad = jnp.concatenate([route_weights.reshape(-1), jnp.zeros((1,), route_weights.dtype)], 0)

    def visit(state_pair, expert):
        token_acc, weight_acc = state_pair
        slot_pairs = slot_table[expert]
        tok_idx = jnp.where(slot_pairs < pair_count, slot_pairs // top_count, token_count).astype(jnp.int32)
        row_terms, weight_grad = expert_grads(token_pad[tok_idx], grad_pad[tok_idx],
                                              w_gate[expert], w_up[expert], w_down[expert])
        slot_weight = weight_pad[slot_pairs]
        token_acc = token_acc.at[tok_idx].add(slot_weight[:, None] * row_terms.astype(jnp.float32))
        weight_acc = weight_acc.at[slot_pairs].set(weight_grad)
        return (token_acc, weight_acc), None

    start_state = (jnp.zeros((token_count + 1, model_width), jnp.float32),
                   jnp.zeros((pair_count + 1,), jnp.bfloat16))
    final_state, unused = lax.scan(visit, start_state, jnp.arange(experts, dtype=jnp.int32))
    token_acc, weight_acc = final_state
    return token_acc[:token_count].astype(jnp.bfloat16), weight_acc[:pair_count].reshape(token_count, top_count)
```

```python
import jax
import jax.numpy as jnp
import numpy as np
from jax import lax
from jax.experimental import pallas as pl
from jax.experimental.pallas import tpu as pltpu
from jax.sharding import PartitionSpec as P

BOTH = ("grp", "ep")
CONTRACT_LAST = (((1,), (1,)), ((), ()))


def expert_grads(rows_in, grads_in, w_gate, w_up, w_down):
    gate_pre = jnp.dot(rows_in, w_gate, preferred_element_type=jnp.float32)
    up_pre = jnp.dot(rows_in, w_up, preferred_element_type=jnp.float32)
    hidden_grad = lax.dot_general(grads_in, w_down, CONTRACT_LAST, preferred_element_type=jnp.float32)
    sigmoid_gate = 1.0 / (1.0 + jnp.exp(-gate_pre))
    activation = gate_pre * sigmoid_gate
    hidden = activation * up_pre
    weight_grad = jnp.sum(hidden_grad * hidden, axis=-1, keepdims=True)
    grad_up = (hidden_grad * activation).astype(jnp.bfloat16)
    grad_gate = (
        hidden_grad * up_pre * sigmoid_gate * (1.0 + gate_pre * (1.0 - sigmoid_gate))
    ).astype(jnp.bfloat16)
    row_terms = (
        lax.dot_general(grad_gate, w_gate, CONTRACT_LAST, preferred_element_type=jnp.float32)
        + lax.dot_general(grad_up, w_up, CONTRACT_LAST, preferred_element_type=jnp.float32)
    ).astype(jnp.bfloat16)
    return (row_terms, weight_grad)


def slot_plan(routes, experts, capacity):
    tok_rows, top_count = routes.shape
    flat_ids = routes.reshape(-1)
    pad_pair = flat_ids.shape[0]
    pair_ids = jnp.arange(pad_pair, dtype=jnp.int32)
    sort_order = jnp.argsort(flat_ids, stable=True)
    sorted_ids = flat_ids[sort_order]
    onehot = (flat_ids[:, None] == jnp.arange(experts, dtype=jnp.int32)[None, :]).astype(jnp.int32)
    counts = jnp.sum(onehot, axis=0)
    starts = jnp.cumsum(counts) - counts
    sorted_rank = pair_ids - starts[sorted_ids]
    sorted_slot = sorted_ids * capacity + sorted_rank
    slot_of_pair = jnp.zeros((pad_pair,), jnp.int32).at[sort_order].set(sorted_slot)
    slot_pair = jnp.full((experts * capacity,), pad_pair, jnp.int32).at[sorted_slot].set(sort_order)
    slot_token = jnp.where(slot_pair < pad_pair, slot_pair // top_count, tok_rows)
    return (slot_of_pair, slot_token)


def place_rows(source_rows, slot_token):
    padded = jnp.concatenate(
        [source_rows, jnp.zeros((1, source_rows.shape[1]), source_rows.dtype)], 0
    )
    return padded[slot_token]


def routed_plan(tokens, cotangent, expert_ids, route_weights, w_gate, w_up, w_down):
    group_count = lax.axis_size("grp")
    lane_count = lax.axis_size("ep")
    experts = group_count * lane_count
    tok_rows, top_count = expert_ids.shape
    model_width = tokens.shape[1]
    capacity = 2 * tok_rows * top_count // experts
    slot_of_pair, slot_token = slot_plan(expert_ids, experts, capacity)
    shape = (group_count, lane_count, capacity)

    def there_and(array, axes):
        for axis in axes:
            at = BOTH.index(axis)
            array = lax.all_to_all(array, axis, split_axis=at, concat_axis=at, tiled=True)
        return array

    rows_in = there_and(place_rows(tokens, slot_token).reshape(shape + (model_width,)), BOTH)
    grads_in = there_and(place_rows(cotangent, slot_token).reshape(shape + (model_width,)), BOTH)
    row_terms, weight_grad = expert_grads(
        rows_in.reshape(-1, model_width),
        grads_in.reshape(-1, model_width),
        w_gate[0],
        w_up[0],
        w_down[0],
    )
    row_terms = there_and(row_terms.reshape(shape + (model_width,)), BOTH[::-1])
    weight_grad = there_and(weight_grad.astype(jnp.bfloat16).reshape(shape), BOTH[::-1])
    row_terms = row_terms.reshape(experts * capacity, model_width)
    weight_grad = weight_grad.reshape(experts * capacity)
    picked = row_terms[slot_of_pair].reshape(tok_rows, top_count, model_width)
    grad_tokens = jnp.sum(route_weights[:, :, None] * picked.astype(jnp.float32), axis=1)
    grad_weights = weight_grad[slot_of_pair].reshape(tok_rows, top_count)
    return (grad_tokens.astype(jnp.bfloat16), grad_weights)


def grads_kernel(blocks, rows, *refs):
    token_refs, refs = refs[:blocks], refs[blocks:]
    grad_refs, refs = refs[:blocks], refs[blocks:]
    share_ref, gate_a, up_a, down_a, gate_b, up_b, down_b, sum_ref, weight_ref = refs
    rows_in = jnp.concatenate([ref[...] for ref in token_refs], 0)
    grads_in = jnp.concatenate([ref[...] for ref in grad_refs], 0)
    total = None
    for at, (gate, up, down) in enumerate(((gate_a, up_a, down_a), (gate_b, up_b, down_b))):
        row_terms, weight_grad = expert_grads(rows_in, grads_in, gate[...], up[...], down[...])
        scaled = share_ref[:, at : at + 1] * row_terms.astype(jnp.float32)
        total = scaled if total is None else total + scaled
        weight_ref[:, at : at + 1] = weight_grad
    sum_ref[...] = total


def block_grads(tokens, grads, shares, weights):
    blocks = len(tokens)
    rows, width = tokens[0].shape
    hidden = weights[0].shape[1]
    return pl.pallas_call(
        lambda *refs: grads_kernel(blocks, rows, *refs),
        out_shape=(
            jax.ShapeDtypeStruct((blocks * rows, width), jnp.float32),
            jax.ShapeDtypeStruct((blocks * rows, 2), jnp.float32),
        ),
        compiler_params=pltpu.CompilerParams(vmem_limit_bytes=32 << 20),
        cost_estimate=pl.CostEstimate(
            flops=2 * 10 * blocks * rows * width * hidden,
            bytes_accessed=12 * width * hidden + 8 * blocks * rows * width,
            transcendentals=2 * blocks * rows * hidden,
        ),
    )(*tokens, *grads, shares, *weights)


def ring_order(chips_x, lanes):
    order = []
    for x in range(chips_x):
        column = [(x, z) for z in range(lanes)]
        order += column if x % 2 == 0 else column[::-1]
    return order


def ring_plan(tokens, cotangent, expert_ids, route_weights, w_gate, w_up, w_down):
    group_count = lax.axis_size("grp")
    lanes = lax.axis_size("ep")
    devices = group_count * lanes
    chips_x = group_count // 2
    rows, top_count = expert_ids.shape
    width = tokens.shape[1]
    order = ring_order(chips_x, lanes)
    chips = len(order)
    far = chips // 2

    def device(place, core):
        x, z = order[place % chips]
        return (2 * x + core) * lanes + z

    place_of = np.zeros((devices,), np.int32)
    core_of = np.zeros((devices,), np.int32)
    for place in range(chips):
        for core in range(2):
            place_of[device(place, core)] = place
            core_of[device(place, core)] = core
    source_table = np.array(
        [[device(int(place_of[d]) - o, int(core_of[d])) for o in range(chips)] for d in range(devices)], np.int32
    )
    offset_table = np.array(
        [
            [(int(place_of[d]) - int(place_of[t])) % chips if core_of[d] == core_of[t] else chips for t in range(devices)]
            for d in range(devices)
        ],
        np.int32,
    )
    ahead = [(device(p, c), device(p + 1, c)) for p in range(chips) for c in range(2)]
    behind = [(device(p, c), device(p - 1, c)) for p in range(chips) for c in range(2)]
    across = [(device(p, c), device(p, 1 - c)) for p in range(chips) for c in range(2)]

    def send(array, pairs):
        return lax.ppermute(array, BOTH, pairs)

    me = lax.axis_index("grp") * lanes + lax.axis_index("ep")
    core = lax.rem(lax.axis_index("grp"), 2)

    got = {0: (tokens, cotangent)}
    token_up = token_down = tokens
    grad_up = grad_down = cotangent
    mine = (w_gate[0], w_up[0], w_down[0])
    for step in range(1, far + 1):
        token_up = send(token_up, ahead)
        grad_down = send(grad_down, behind)
        if step < far:
            grad_up = send(grad_up, ahead)
            token_down = send(token_down, behind)
            got[step] = (token_up, grad_up)
            got[chips - step] = (token_down, grad_down)
        else:
            got[far] = (token_up, grad_down)
        if step == 1:
            other = tuple(send(w, across) for w in mine)

    expert_list = jnp.arange(devices, dtype=jnp.int32)
    chosen = expert_ids[None, :, :] == expert_list[:, None, None]
    dense = jnp.sum(jnp.where(chosen, route_weights[None], 0.0), axis=-1)
    dense = dense.reshape(chips_x, 1, 2, lanes, rows).transpose(0, 1, 3, 2, 4)
    dense = jnp.broadcast_to(dense, (chips_x, 2, lanes, 2, rows)).reshape(devices, 2, rows)
    dense = lax.all_to_all(dense, BOTH, split_axis=0, concat_axis=0, tiled=True)
    shares = jnp.take(dense, jnp.asarray(source_table)[me], axis=0)
    shares = jnp.where(core == 0, shares, shares[:, ::-1]).transpose(0, 2, 1)

    sums, weight_grads = {}, {}
    for step in range(far + 1):
        offsets = (step,) if step in (0, far) else (step, chips - step)
        total, weight_grad = block_grads(
            [got[o][0] for o in offsets],
            [got[o][1] for o in offsets],
            jnp.concatenate([shares[o] for o in offsets], 0),
            mine + other,
        )
        for at, o in enumerate(offsets):
            sums[o] = total[at * rows : (at + 1) * rows]
            weight_grads[o] = weight_grad[at * rows : (at + 1) * rows]

    half = width // 2
    halves = (slice(0, half), slice(half, width))

    def chain(columns, pairs, offsets):
        moving = sums[offsets[0]][:, columns].astype(jnp.bfloat16)
        for o in offsets[1:]:
            moving = send(moving, pairs)
            moving = (moving.astype(jnp.float32) + sums[o][:, columns]).astype(jnp.bfloat16)
        return send(moving, pairs).astype(jnp.float32)

    up_way = [(chips - s) for s in range(far, 0, -1)]
    down_way = list(range(far, 0, -1))
    back = [
        sums[0][:, halves[0]] + chain(halves[0], ahead, up_way) + chain(halves[0], behind, down_way[1:]),
        sums[0][:, halves[1]] + chain(halves[1], ahead, up_way[1:]) + chain(halves[1], behind, down_way),
    ]
    grad_tokens = jnp.concatenate(back, 1).astype(jnp.bfloat16)

    by_offset = jnp.stack([weight_grads[o] for o in range(chips)] + [jnp.zeros((rows, 2), jnp.float32)])
    by_offset = by_offset.transpose(0, 2, 1).astype(jnp.bfloat16)
    by_offset = jnp.where(core == 0, by_offset, by_offset[:, ::-1])
    outgoing = jnp.take(by_offset, jnp.asarray(offset_table)[me], axis=0)
    incoming = lax.all_to_all(outgoing, BOTH, split_axis=0, concat_axis=0, tiled=True)
    incoming = incoming.reshape(chips_x, 2, lanes, 2, rows).sum(axis=1)
    incoming = incoming.transpose(0, 2, 1, 3).reshape(devices, rows)
    grad_weights = jnp.sum(jnp.where(chosen, incoming[:, :, None], 0), axis=0)
    return (grad_tokens, grad_weights.astype(jnp.bfloat16))


def on_device(tokens, cotangent, expert_ids, route_weights, w_gate, w_up, w_down):
    group_count = lax.axis_size("grp")
    experts = group_count * lax.axis_size("ep")
    rows, top_count = expert_ids.shape
    capacity = 2 * rows * top_count // experts
    dense = 2 * capacity >= rows and group_count % 2 == 0
    plan = ring_plan if dense else routed_plan
    return plan(tokens, cotangent, expert_ids, route_weights, w_gate, w_up, w_down)


def solution(mesh):
    in_specs = (
        P(("parts", "grp", "ep"), None),
        P(("parts", "grp", "ep"), None),
        P(("parts", "grp", "ep"), None),
        P(("parts", "grp", "ep"), None),
        P(("grp", "ep"), None, None),
        P(("grp", "ep"), None, None),
        P(("grp", "ep"), None, None),
    )
    out_specs = (P(("parts", "grp", "ep"), None), P(("parts", "grp", "ep"), None))
    return jax.shard_map(
        on_device, mesh=mesh, in_specs=in_specs, out_specs=out_specs, check_vma=False
    )
```

```python
import jax
import jax.numpy as jnp
import numpy as np
from jax import lax
from jax.experimental import pallas as pl
from jax.experimental.pallas import tpu as pltpu
from jax.sharding import PartitionSpec as P

BOTH = ("grp", "ep")
CONTRACT_LAST = (((1,), (1,)), ((), ()))


def expert_grads(rows_in, grads_in, w_gate, w_up, w_down):
    gate_pre = jnp.dot(rows_in, w_gate, preferred_element_type=jnp.float32)
    up_pre = jnp.dot(rows_in, w_up, preferred_element_type=jnp.float32)
    hidden_grad = lax.dot_general(grads_in, w_down, CONTRACT_LAST, preferred_element_type=jnp.float32)
    sigmoid_gate = 1.0 / (1.0 + jnp.exp(-gate_pre))
    activation = gate_pre * sigmoid_gate
    hidden = activation * up_pre
    weight_grad = jnp.sum(hidden_grad * hidden, axis=-1, keepdims=True)
    grad_up = (hidden_grad * activation).astype(jnp.bfloat16)
    grad_gate = (
        hidden_grad * up_pre * sigmoid_gate * (1.0 + gate_pre * (1.0 - sigmoid_gate))
    ).astype(jnp.bfloat16)
    row_terms = (
        lax.dot_general(grad_gate, w_gate, CONTRACT_LAST, preferred_element_type=jnp.float32)
        + lax.dot_general(grad_up, w_up, CONTRACT_LAST, preferred_element_type=jnp.float32)
    ).astype(jnp.bfloat16)
    return (row_terms, weight_grad)


def slot_plan(routes, experts, capacity):
    tok_rows, top_count = routes.shape
    flat_ids = routes.reshape(-1)
    pad_pair = flat_ids.shape[0]
    pair_ids = jnp.arange(pad_pair, dtype=jnp.int32)
    sort_order = jnp.argsort(flat_ids, stable=True)
    sorted_ids = flat_ids[sort_order]
    onehot = (flat_ids[:, None] == jnp.arange(experts, dtype=jnp.int32)[None, :]).astype(jnp.int32)
    counts = jnp.sum(onehot, axis=0)
    starts = jnp.cumsum(counts) - counts
    sorted_rank = pair_ids - starts[sorted_ids]
    sorted_slot = sorted_ids * capacity + sorted_rank
    slot_of_pair = jnp.zeros((pad_pair,), jnp.int32).at[sort_order].set(sorted_slot)
    slot_pair = jnp.full((experts * capacity,), pad_pair, jnp.int32).at[sorted_slot].set(sort_order)
    slot_token = jnp.where(slot_pair < pad_pair, slot_pair // top_count, tok_rows)
    return (slot_of_pair, slot_token)


def place_rows(source_rows, slot_token):
    padded = jnp.concatenate(
        [source_rows, jnp.zeros((1, source_rows.shape[1]), source_rows.dtype)], 0
    )
    return padded[slot_token]


def routed_plan(tokens, cotangent, expert_ids, route_weights, w_gate, w_up, w_down):
    group_count = lax.axis_size("grp")
    lane_count = lax.axis_size("ep")
    experts = group_count * lane_count
    tok_rows, top_count = expert_ids.shape
    model_width = tokens.shape[1]
    capacity = 2 * tok_rows * top_count // experts
    slot_of_pair, slot_token = slot_plan(expert_ids, experts, capacity)
    shape = (group_count, lane_count, capacity)

    def there_and(array, axes):
        for axis in axes:
            at = BOTH.index(axis)
            array = lax.all_to_all(array, axis, split_axis=at, concat_axis=at, tiled=True)
        return array

    rows_in = there_and(place_rows(tokens, slot_token).reshape(shape + (model_width,)), BOTH)
    grads_in = there_and(place_rows(cotangent, slot_token).reshape(shape + (model_width,)), BOTH)
    row_terms, weight_grad = expert_grads(
        rows_in.reshape(-1, model_width),
        grads_in.reshape(-1, model_width),
        w_gate[0],
        w_up[0],
        w_down[0],
    )
    row_terms = there_and(row_terms.reshape(shape + (model_width,)), BOTH[::-1])
    weight_grad = there_and(weight_grad.astype(jnp.bfloat16).reshape(shape), BOTH[::-1])
    row_terms = row_terms.reshape(experts * capacity, model_width)
    weight_grad = weight_grad.reshape(experts * capacity)
    picked = row_terms[slot_of_pair].reshape(tok_rows, top_count, model_width)
    grad_tokens = jnp.sum(route_weights[:, :, None] * picked.astype(jnp.float32), axis=1)
    grad_weights = weight_grad[slot_of_pair].reshape(tok_rows, top_count)
    return (grad_tokens.astype(jnp.bfloat16), grad_weights)


def after(array, *others):
    return lax.optimization_barrier((array,) + others)[0]


def spread_experts(column, row_of, extra):
    rows = column.shape[0]
    across = lax.broadcasted_iota(jnp.int32, (rows, rows), 1)
    down = lax.broadcasted_iota(jnp.int32, (rows, rows), 0)
    line = jnp.sum(jnp.where(across == down, column, 0.0), axis=0, keepdims=True)
    return jnp.where(lax.broadcasted_iota(jnp.int32, (extra, rows), 0) == row_of, line, 0.0)


def grads_kernel(blocks, rows, extra, *refs):
    place_ref, refs = refs[0], refs[1:]
    token_refs, refs = refs[:blocks], refs[blocks:]
    grad_refs, refs = refs[:blocks], refs[blocks:]
    share_refs, refs = refs[:blocks], refs[blocks:]
    weights, outs = (refs[:3], refs[3:6]), refs[6:]
    rows_in = jnp.concatenate([ref[...] for ref in token_refs], 0)
    grads_in = jnp.concatenate([ref[...] for ref in grad_refs], 0)
    shares = jnp.concatenate([ref[...] for ref in share_refs], 0)
    total, spread = None, [None] * blocks
    for at, (gate, up, down) in enumerate(weights):
        row_terms, weight_grad = expert_grads(rows_in, grads_in, gate[...], up[...], down[...])
        scaled = shares[:, at : at + 1] * row_terms.astype(jnp.float32)
        total = scaled if total is None else total + scaled
        for i in range(blocks):
            lines = spread_experts(weight_grad[i * rows : (i + 1) * rows], place_ref[at], extra)
            spread[i] = lines if at == 0 else spread[i] + lines
    half = total.shape[1] // 2
    for i in range(blocks):
        left, right = outs[2 * i], outs[2 * i + 1]
        block = total[i * rows : (i + 1) * rows]
        left[:rows, :] = block[:, :half].astype(left.dtype)
        left[rows:, :] = jnp.zeros((extra, half), left.dtype)
        left[rows:, :rows] = spread[i].astype(jnp.bfloat16).astype(left.dtype)
        right[...] = block[:, half:].astype(right.dtype)


def block_grads(places, blocks_in, weights, extra, kinds):
    tokens, grads, shares = zip(*blocks_in)
    blocks = len(tokens)
    rows, width = tokens[0].shape
    hidden = weights[0].shape[1]
    outs = []
    for left, right in kinds:
        outs.append(jax.ShapeDtypeStruct((rows + extra, width // 2), left))
        outs.append(jax.ShapeDtypeStruct((rows, width // 2), right))
    vmem = pl.BlockSpec(memory_space=pltpu.VMEM)
    out = pl.pallas_call(
        lambda *refs: grads_kernel(blocks, rows, extra, *refs),
        in_specs=[pl.BlockSpec(memory_space=pltpu.SMEM)] + [vmem] * (3 * blocks + 6),
        out_shape=outs,
        compiler_params=pltpu.CompilerParams(vmem_limit_bytes=24 << 20),
        cost_estimate=pl.CostEstimate(
            flops=2 * 10 * blocks * rows * width * hidden,
            bytes_accessed=12 * width * hidden + 8 * blocks * rows * width,
            transcendentals=2 * blocks * rows * hidden,
        ),
    )(places, *tokens, *grads, *shares, *weights)
    return [(out[2 * i], out[2 * i + 1]) for i in range(blocks)]


def add_kernel(*refs):
    count = len(refs) // 3
    for i in range(count):
        came, own, out = refs[2 * i], refs[2 * i + 1], refs[2 * count + i]
        out[...] = (came[...].astype(jnp.float32) + own[...]).astype(out.dtype)


def add_pairs(*pairs):
    operands = [array for pair in pairs for array in pair]
    return pl.pallas_call(
        add_kernel,
        out_shape=[jax.ShapeDtypeStruct(came.shape, came.dtype) for came, own in pairs],
        compiler_params=pltpu.CompilerParams(vmem_limit_bytes=8 << 20),
    )(*operands)


def finish_kernel(left_own, right_own, left_a, left_b, right_a, right_b, ids, tokens_out, weights_out):
    rows, half = right_own.shape
    extra = left_own.shape[0] - rows
    as_f32 = lambda ref: ref[...].astype(jnp.float32)
    left = left_own[...] + as_f32(left_a) + as_f32(left_b)
    tokens_out[:, :half] = left[:rows].astype(tokens_out.dtype)
    tokens_out[:, half:] = (right_own[...] + as_f32(right_a) + as_f32(right_b)).astype(tokens_out.dtype)
    grads = left[rows:, :rows]
    by_token = jnp.concatenate([grads, jnp.zeros((rows - extra, rows), jnp.float32)], 0).T
    lanes = lax.broadcasted_iota(jnp.int32, (rows, rows), 1)
    for k in range(ids.shape[1]):
        picked = jnp.where(lanes == ids[:, k : k + 1], by_token, 0.0)
        weights_out[:, k : k + 1] = jnp.sum(picked, axis=1, keepdims=True).astype(weights_out.dtype)


def ring_order(chips_x, lanes):
    order = []
    for x in range(chips_x):
        column = [(x, z) for z in range(lanes)]
        order += column if x % 2 == 0 else column[::-1]
    return order


def ring_plan(tokens, cotangent, expert_ids, route_weights, w_gate, w_up, w_down):
    group_count = lax.axis_size("grp")
    lanes = lax.axis_size("ep")
    devices = group_count * lanes
    rows, top_count = expert_ids.shape
    order = ring_order(group_count // 2, lanes)
    chips = len(order)
    far = chips // 2
    extra = -(-devices // 16) * 16

    def device(place, core):
        x, z = order[place % chips]
        return (2 * x + core) * lanes + z

    source_table = np.zeros((devices, chips), np.int32)
    other_table = np.zeros((devices,), np.int32)
    for place in range(chips):
        for core in range(2):
            source_table[device(place, core)] = [device(place - o, core) for o in range(chips)]
            other_table[device(place, core)] = device(place, 1 - core)
    ahead = [(device(p, c), device(p + 1, c)) for p in range(chips) for c in range(2)]
    behind = [(device(p, c), device(p - 1, c)) for p in range(chips) for c in range(2)]
    across = [(device(p, c), device(p, 1 - c)) for p in range(chips) for c in range(2)]

    def send(array, pairs):
        return lax.ppermute(array, BOTH, pairs)

    me = lax.axis_index("grp") * lanes + lax.axis_index("ep")
    places = jnp.stack([me, jnp.asarray(other_table)[me]])

    token_up, token_down = send(tokens, ahead), send(tokens, behind)
    expert_list = jnp.arange(devices, dtype=jnp.int32)
    chosen = expert_ids[None, :, :] == expert_list[:, None, None]
    dense = jnp.sum(jnp.where(chosen, route_weights[None], 0.0), axis=-1)
    later = after(cotangent, dense)
    grad_up, grad_down = send(later, ahead), send(later, behind)
    mine = (w_gate[0], w_up[0], w_down[0])
    weights = mine + tuple(send(w, across) for w in mine)

    shares = lax.all_gather(dense, BOTH)[jnp.asarray(source_table)[me]]
    shares = jnp.take(shares, places, axis=1).transpose(0, 2, 1)

    sums = {}

    def compute(blocks):
        kinds = []
        for o, *unused in blocks:
            left = jnp.bfloat16 if o in (far, far - 1) else jnp.float32
            right = jnp.bfloat16 if o in (far, chips - far + 1) else jnp.float32
            kinds.append((left, right))
        out = block_grads(places, [(t, g, shares[o]) for o, t, g in blocks], weights, extra, kinds)
        for (o, *unused), pair in zip(blocks, out):
            sums[o] = pair

    compute([(0, tokens, cotangent)])
    got = [(1, token_up, grad_up), (chips - 1, token_down, grad_down)]
    for step in range(2, far):
        if step > 2:
            token_up = after(token_up, sums[step - 2][0])
            token_down = after(token_down, sums[step - 2][0])
        token_up, token_down = send(token_up, ahead), send(token_down, behind)
        grad_up, grad_down = send(grad_up, ahead), send(grad_down, behind)
        compute(got)
        got = [(step, token_up, grad_up), (chips - step, token_down, grad_down)]
    token_up = after(token_up, sums[far - 2][0])
    grad_down = after(grad_down, sums[far - 2][0])
    token_up, grad_down = send(token_up, ahead), send(grad_down, behind)
    compute(got)

    right_up, left_down = sums[chips - far + 1][1], sums[far - 1][0]
    right_up, left_down = send(right_up, ahead), send(left_down, behind)
    compute([(far, token_up, grad_down)])
    left_up, right_down = sums[far]
    for step in range(far, 0, -1):
        left_up, right_down = send(left_up, ahead), send(right_down, behind)
        if step > 2:
            right_up, left_down = add_pairs((right_up, sums[chips - step + 2][1]), (left_down, sums[step - 2][0]))
            right_up, left_down = send(right_up, ahead), send(left_down, behind)
        if step > 1:
            left_up, right_down = add_pairs((left_up, sums[chips - step + 1][0]), (right_down, sums[step - 1][1]))

    return pl.pallas_call(
        finish_kernel,
        out_shape=[
            jax.ShapeDtypeStruct(tokens.shape, tokens.dtype),
            jax.ShapeDtypeStruct(expert_ids.shape, jnp.bfloat16),
        ],
        compiler_params=pltpu.CompilerParams(vmem_limit_bytes=8 << 20),
    )(*sums[0], left_up, left_down, right_up, right_down, expert_ids)


def on_device(tokens, cotangent, expert_ids, route_weights, w_gate, w_up, w_down):
    group_count = lax.axis_size("grp")
    experts = group_count * lax.axis_size("ep")
    rows, top_count = expert_ids.shape
    capacity = 2 * rows * top_count // experts
    fits = rows % 128 == 0 and experts <= rows <= tokens.shape[1] // 2 and group_count % 2 == 0 and experts >= 8
    plan = ring_plan if fits and 2 * capacity >= rows else routed_plan
    return plan(tokens, cotangent, expert_ids, route_weights, w_gate, w_up, w_down)


def solution(mesh):
    in_specs = (
        P(("parts", "grp", "ep"), None),
        P(("parts", "grp", "ep"), None),
        P(("parts", "grp", "ep"), None),
        P(("parts", "grp", "ep"), None),
        P(("grp", "ep"), None, None),
        P(("grp", "ep"), None, None),
        P(("grp", "ep"), None, None),
    )
    out_specs = (P(("parts", "grp", "ep"), None), P(("parts", "grp", "ep"), None))
    return jax.shard_map(
        on_device, mesh=mesh, in_specs=in_specs, out_specs=out_specs, check_vma=False
    )
```

```python
import jax
import jax.numpy as jnp
from jax import lax
from jax.experimental import pallas as pl
from jax.experimental.pallas import tpu as pltpu
from jax.sharding import PartitionSpec as P

BOTH = ("grp", "ep")
LIGHT = pl.CostEstimate(flops=0, transcendentals=0, bytes_accessed=0)
CONTRACT_LAST = (((1,), (1,)), ((), ()))


def expert_grads(rows_in, grads_in, w_gate, w_up, w_down):
    gate_pre = jnp.dot(rows_in, w_gate, preferred_element_type=jnp.float32)
    up_pre = jnp.dot(rows_in, w_up, preferred_element_type=jnp.float32)
    hidden_grad = lax.dot_general(grads_in, w_down, CONTRACT_LAST, preferred_element_type=jnp.float32)
    grad_gate, grad_up, weight_grad = hidden_grads(gate_pre, up_pre, hidden_grad)
    return (both_terms(grad_gate, grad_up, w_gate, w_up), weight_grad)


def both_terms(grad_gate, grad_up, w_gate, w_up):
    row_terms = lax.dot_general(grad_gate, w_gate, CONTRACT_LAST, preferred_element_type=jnp.float32)
    row_terms += lax.dot_general(grad_up, w_up, CONTRACT_LAST, preferred_element_type=jnp.float32)
    return row_terms.astype(jnp.bfloat16)


def hidden_grads(gate_pre, up_pre, hidden_grad):
    sigmoid_gate = 1.0 / (1.0 + jnp.exp(-gate_pre))
    activation = gate_pre * sigmoid_gate
    hidden = activation * up_pre
    weight_grad = jnp.sum(hidden_grad * hidden, axis=-1, keepdims=True)
    grad_up = (hidden_grad * activation).astype(jnp.bfloat16)
    grad_gate = (
        hidden_grad * up_pre * sigmoid_gate * (1.0 + gate_pre * (1.0 - sigmoid_gate))
    ).astype(jnp.bfloat16)
    return (grad_gate, grad_up, weight_grad)


def slot_plan(routes, experts, capacity):
    tok_rows, top_count = routes.shape
    flat_ids = routes.reshape(-1)
    pad_pair = flat_ids.shape[0]
    pair_ids = jnp.arange(pad_pair, dtype=jnp.int32)
    sort_order = jnp.argsort(flat_ids, stable=True)
    sorted_ids = flat_ids[sort_order]
    onehot = (flat_ids[:, None] == jnp.arange(experts, dtype=jnp.int32)[None, :]).astype(jnp.int32)
    counts = jnp.sum(onehot, axis=0)
    starts = jnp.cumsum(counts) - counts
    sorted_rank = pair_ids - starts[sorted_ids]
    sorted_slot = sorted_ids * capacity + sorted_rank
    slot_of_pair = jnp.zeros((pad_pair,), jnp.int32).at[sort_order].set(sorted_slot)
    slot_pair = jnp.full((experts * capacity,), pad_pair, jnp.int32).at[sorted_slot].set(sort_order)
    slot_token = jnp.where(slot_pair < pad_pair, slot_pair // top_count, tok_rows)
    return (slot_of_pair, slot_token)


def place_rows(source_rows, slot_token):
    padded = jnp.concatenate(
        [source_rows, jnp.zeros((1, source_rows.shape[1]), source_rows.dtype)], 0
    )
    return padded[slot_token]


def routed_plan(tokens, cotangent, expert_ids, route_weights, w_gate, w_up, w_down):
    group_count = lax.axis_size("grp")
    lane_count = lax.axis_size("ep")
    experts = group_count * lane_count
    tok_rows, top_count = expert_ids.shape
    model_width = tokens.shape[1]
    capacity = 2 * tok_rows * top_count // experts
    slot_of_pair, slot_token = slot_plan(expert_ids, experts, capacity)
    shape = (group_count, lane_count, capacity)

    def there_and(array, axes):
        for axis in axes:
            at = BOTH.index(axis)
            array = lax.all_to_all(array, axis, split_axis=at, concat_axis=at, tiled=True)
        return array

    rows_in = there_and(place_rows(tokens, slot_token).reshape(shape + (model_width,)), BOTH)
    grads_in = there_and(place_rows(cotangent, slot_token).reshape(shape + (model_width,)), BOTH)
    row_terms, weight_grad = expert_grads(
        rows_in.reshape(-1, model_width),
        grads_in.reshape(-1, model_width),
        w_gate[0],
        w_up[0],
        w_down[0],
    )
    row_terms = there_and(row_terms.reshape(shape + (model_width,)), BOTH[::-1])
    weight_grad = there_and(weight_grad.astype(jnp.bfloat16).reshape(shape), BOTH[::-1])
    row_terms = row_terms.reshape(experts * capacity, model_width)
    weight_grad = weight_grad.reshape(experts * capacity)
    picked = row_terms[slot_of_pair].reshape(tok_rows, top_count, model_width)
    grad_tokens = jnp.sum(route_weights[:, :, None] * picked.astype(jnp.float32), axis=1)
    grad_weights = weight_grad[slot_of_pair].reshape(tok_rows, top_count)
    return (grad_tokens.astype(jnp.bfloat16), grad_weights)


def after_all(*arrays):
    return lax.optimization_barrier(arrays)


def spread_experts(column, row_of, extra):
    rows = column.shape[0]
    across = lax.broadcasted_iota(jnp.int32, (rows, rows), 1)
    down = lax.broadcasted_iota(jnp.int32, (rows, rows), 0)
    line = jnp.sum(jnp.where(across == down, column, 0.0), axis=0, keepdims=True)
    return jnp.where(lax.broadcasted_iota(jnp.int32, (extra, rows), 0) == row_of, line, 0.0)


def bf16_pieces(values):
    pieces = []
    for unused in range(3):
        piece = values.astype(jnp.bfloat16)
        values = values - piece.astype(jnp.float32)
        pieces.append(piece)
    return pieces


def read_share(lines, expert, experts, rows):
    pieces = lines.astype(jnp.float32)
    groups = pieces.shape[1] // rows
    slot = lax.broadcasted_iota(jnp.int32, pieces.shape, 0) * groups
    slot = slot + lax.broadcasted_iota(jnp.int32, pieces.shape, 1) // rows
    wanted = (slot == expert) | (slot == expert + experts) | (slot == expert + 2 * experts)
    kept = jnp.where(wanted, pieces, 0.0)
    line = sum(kept[:, g * rows : (g + 1) * rows] for g in range(groups))
    line = jnp.sum(line, axis=0, keepdims=True)
    across = lax.broadcasted_iota(jnp.int32, (rows, rows), 1)
    down = lax.broadcasted_iota(jnp.int32, (rows, rows), 0)
    return jnp.sum(jnp.where(across == down, line, 0.0), axis=1, keepdims=True)


def merge_kernel(gate, up, down, out):
    hidden = gate.shape[1]
    out[:, :hidden] = gate[...]
    out[:, hidden : 2 * hidden] = up[...]
    out[:, 2 * hidden :] = down[...].T


def merge_weights(w_gate, w_up, w_down):
    return pl.pallas_call(
        merge_kernel,
        out_shape=pltpu.HBM((w_gate.shape[0], 3 * w_gate.shape[1]), w_gate.dtype),
        compiler_params=pltpu.CompilerParams(vmem_limit_bytes=24 << 20),
        cost_estimate=LIGHT,
    )(w_gate, w_up, w_down)


def hold_kernel(count, pieces, *refs):
    sources, held, sems = refs[:count], refs[count : 2 * count], refs[-1]
    copies = []
    for at in range(count):
        rows = sources[at].shape[0] // pieces
        for i in range(pieces):
            part = pl.ds(i * rows, rows)
            copies.append(pltpu.make_async_copy(sources[at].at[part], held[at].at[part], sems.at[at, i]))
    for copy in copies:
        copy.start()
    for copy in copies:
        copy.wait()


def hold(*arrays, pieces=4):
    return pl.pallas_call(
        lambda *refs: hold_kernel(len(arrays), pieces, *refs),
        in_specs=[pl.BlockSpec(memory_space=pl.ANY)] * len(arrays),
        out_shape=[pltpu.VMEM(array.shape, array.dtype) for array in arrays],
        scratch_shapes=[pltpu.SemaphoreType.DMA((len(arrays), pieces))],
        compiler_params=pltpu.CompilerParams(vmem_limit_bytes=24 << 20),
        cost_estimate=LIGHT,
    )(*arrays)


def grads_kernel(blocks, rows, experts, extra, *refs):
    place_ref, refs = refs[0], refs[1:]
    token_refs, grad_refs, refs = refs[:blocks], refs[blocks : 2 * blocks], refs[2 * blocks :]
    weights, outs = refs[:2], refs[2:]
    places = [jnp.max(place_ref[:, at : at + 1]) for at in range(2)]
    rows_in = jnp.concatenate([ref[...] for ref in token_refs], 0)
    with_lines = [ref[...] for ref in grad_refs]
    grads_in = jnp.concatenate([block[:rows] for block in with_lines], 0)
    total, spread = None, [None] * blocks
    for at, merged in enumerate(weights):
        hidden = merged.shape[1] // 3
        w_gate, w_up, w_down = (merged[:, i * hidden : (i + 1) * hidden] for i in range(3))
        gate_pre = jnp.dot(rows_in, w_gate, preferred_element_type=jnp.float32)
        up_pre = jnp.dot(rows_in, w_up, preferred_element_type=jnp.float32)
        hidden_grad = jnp.dot(grads_in, w_down, preferred_element_type=jnp.float32)
        grad_gate, grad_up, weight_grad = hidden_grads(gate_pre, up_pre, hidden_grad)
        row_terms = both_terms(grad_gate, grad_up, w_gate, w_up)
        shares = [read_share(block[rows:], places[at], experts, rows) for block in with_lines]
        scaled = jnp.concatenate(shares, 0) * row_terms.astype(jnp.float32)
        total = scaled if total is None else total + scaled
        for i in range(blocks):
            lines = spread_experts(weight_grad[i * rows : (i + 1) * rows], places[at], extra)
            spread[i] = lines if at == 0 else spread[i] + lines
    half = total.shape[1] // 2
    for i in range(blocks):
        left, right = outs[2 * i], outs[2 * i + 1]
        block = total[i * rows : (i + 1) * rows]
        left[:rows, :] = block[:, :half].astype(left.dtype)
        left[rows:, :] = jnp.zeros((extra, half), left.dtype)
        left[rows:, :rows] = spread[i].astype(jnp.bfloat16).astype(left.dtype)
        right[...] = block[:, half:].astype(right.dtype)


def block_grads(places, blocks_in, weights, experts, extra, kinds):
    tokens, grads = zip(*blocks_in)
    blocks = len(tokens)
    rows, width = tokens[0].shape
    outs = []
    for left, right in kinds:
        outs.append(jax.ShapeDtypeStruct((rows + extra, width // 2), left))
        outs.append(jax.ShapeDtypeStruct((rows, width // 2), right))
    weights = [pltpu.with_memory_space_constraint(w, pltpu.VMEM) for w in weights]
    out = pl.pallas_call(
        lambda *refs: grads_kernel(blocks, rows, experts, extra, *refs),
        out_shape=outs,
        compiler_params=pltpu.CompilerParams(vmem_limit_bytes=24 << 20),
        cost_estimate=LIGHT,
    )(places, *tokens, *grads, *weights)
    return [(out[2 * i], out[2 * i + 1]) for i in range(blocks)]


def add_kernel(*refs):
    count = len(refs) // 3
    for i in range(count):
        came, own, out = refs[2 * i], refs[2 * i + 1], refs[2 * count + i]
        out[...] = (came[...].astype(jnp.float32) + own[...]).astype(out.dtype)


def add_pairs(*pairs):
    operands = [array for pair in pairs for array in pair]
    return pl.pallas_call(
        add_kernel,
        out_shape=[jax.ShapeDtypeStruct(came.shape, came.dtype) for came, own in pairs],
        compiler_params=pltpu.CompilerParams(vmem_limit_bytes=8 << 20),
        cost_estimate=LIGHT,
    )(*operands)


def finish_kernel(left_own, right_own, left_a, left_b, right_a, right_b, ids, tokens_out, weights_out):
    rows, half = right_own.shape
    extra = left_own.shape[0] - rows
    as_f32 = lambda ref: ref[...].astype(jnp.float32)
    left = left_own[...] + as_f32(left_a) + as_f32(left_b)
    tokens_out[:, :half] = left[:rows].astype(tokens_out.dtype)
    tokens_out[:, half:] = (right_own[...] + as_f32(right_a) + as_f32(right_b)).astype(tokens_out.dtype)
    grads = left[rows:, :rows]
    by_token = jnp.concatenate([grads, jnp.zeros((rows - extra, rows), jnp.float32)], 0).T
    lanes = lax.broadcasted_iota(jnp.int32, (rows, rows), 1)
    for k in range(ids.shape[1]):
        picked = jnp.where(lanes == ids[:, k : k + 1], by_token, 0.0)
        weights_out[:, k : k + 1] = jnp.sum(picked, axis=1, keepdims=True).astype(weights_out.dtype)


def ring_order(chips_x, lanes):
    order = []
    for x in range(chips_x):
        column = [(x, z) for z in range(lanes)]
        order += column if x % 2 == 0 else column[::-1]
    return order


def ring_plan(tokens, cotangent, expert_ids, route_weights, w_gate, w_up, w_down):
    group_count = lax.axis_size("grp")
    lanes = lax.axis_size("ep")
    devices = group_count * lanes
    rows, width = tokens.shape
    order = ring_order(group_count // 2, lanes)
    chips = len(order)
    far = chips // 2
    extra = -(-devices // 16) * 16

    def device(place, core):
        x, z = order[place % chips]
        return (2 * x + core) * lanes + z

    ahead = [(device(p, c), device(p + 1, c)) for p in range(chips) for c in range(2)]
    behind = [(device(p, c), device(p - 1, c)) for p in range(chips) for c in range(2)]
    across = [(device(p, c), device(p, 1 - c)) for p in range(chips) for c in range(2)]

    def send(array, pairs):
        return lax.ppermute(array, BOTH, pairs)

    me = lax.axis_index("grp") * lanes + lax.axis_index("ep")
    other = jnp.where(lax.rem(lax.axis_index("grp"), 2) == 0, me + lanes, me - lanes)
    places = jnp.stack([me, other]).reshape(1, 2)

    token_up, token_down = send(tokens, ahead), send(tokens, behind)
    expert_list = jnp.arange(devices, dtype=jnp.int32)
    chosen = expert_ids[None, :, :] == expert_list[:, None, None]
    dense = jnp.sum(jnp.where(chosen, route_weights[None], 0.0), axis=-1)
    lines = jnp.concatenate(bf16_pieces(dense), 0)
    line_rows = -(-3 * devices * rows // (8 * width)) * 8
    lines = jnp.pad(lines, ((0, line_rows * width // rows - 3 * devices), (0, 0))).reshape(line_rows, width)
    cotangent = jnp.concatenate([cotangent, lines], 0)
    grad_up, grad_down = send(cotangent, ahead), send(cotangent, behind)
    mine = merge_weights(w_gate[0], w_up[0], w_down[0])
    mine = after_all(mine, token_up, token_down, grad_up, grad_down)[0]
    weights = hold(mine, send(mine, across))

    sums = {}

    def compute(blocks):
        kinds = []
        for o, *unused in blocks:
            left = jnp.bfloat16 if o in (far, far - 1) else jnp.float32
            right = jnp.bfloat16 if o in (far, chips - far + 1) else jnp.float32
            kinds.append((left, right))
        out = block_grads(places, [(t, g) for o, t, g in blocks], weights, devices, extra, kinds)
        for (o, *unused), pair in zip(blocks, out):
            sums[o] = pair
        return out[0][0]

    arrived = [[(0, tokens, cotangent)], [(1, token_up, grad_up), (chips - 1, token_down, grad_down)]]
    for step in range(2, far):
        if step == far - 1:
            token_up, token_down = after_all(token_up, token_down, weights[0])[:2]
            grad_up, grad_down = after_all(grad_up, grad_down, compute(arrived[0]))[:2]
        token_up, token_down = send(token_up, ahead), send(token_down, behind)
        grad_up, grad_down = send(grad_up, ahead), send(grad_down, behind)
        arrived.append([(step, token_up, grad_up), (chips - step, token_down, grad_down)])
    token_up = after_all(token_up, compute(arrived[far - 2]))[0]
    token_up, grad_down = send(token_up, ahead), send(grad_down, behind)
    last = compute(arrived[far - 1])

    right_up, left_down = send(sums[chips - far + 1][1], ahead), send(sums[far - 1][0], behind)
    token_up = after_all(token_up, last)[0]
    compute([(far, token_up, grad_down)])
    for o in range(far - 3, 0, -1):
        compute(arrived[o])
    left_up, right_down = after_all(*sums[far], right_up, left_down)[:2]
    for step in range(far, 0, -1):
        left_up, right_down = send(left_up, ahead), send(right_down, behind)
        if step > 2:
            right_up, left_down = add_pairs((right_up, sums[chips - step + 2][1]), (left_down, sums[step - 2][0]))
            turn = right_up
            right_up, left_down = send(right_up, ahead), send(left_down, behind)
        if step > 1:
            left_up, right_down = after_all(left_up, right_down, turn)[:2]
            left_up, right_down = add_pairs((left_up, sums[chips - step + 1][0]), (right_down, sums[step - 1][1]))
            right_up, left_down = after_all(right_up, left_down, left_up)[:2]

    return pl.pallas_call(
        finish_kernel,
        out_shape=[
            jax.ShapeDtypeStruct(tokens.shape, tokens.dtype),
            jax.ShapeDtypeStruct(expert_ids.shape, jnp.bfloat16),
        ],
        compiler_params=pltpu.CompilerParams(vmem_limit_bytes=8 << 20),
    )(*sums[0], left_up, left_down, right_up, right_down, expert_ids)


def on_device(tokens, cotangent, expert_ids, route_weights, w_gate, w_up, w_down):
    group_count = lax.axis_size("grp")
    experts = group_count * lax.axis_size("ep")
    rows, top_count = expert_ids.shape
    capacity = 2 * rows * top_count // experts
    fits = rows % 128 == 0 and experts <= rows <= tokens.shape[1] // 2 and group_count % 2 == 0 and experts >= 8 and tokens.shape[1] % rows == 0
    plan = ring_plan if fits and 2 * capacity >= rows else routed_plan
    return plan(tokens, cotangent, expert_ids, route_weights, w_gate, w_up, w_down)


def solution(mesh):
    in_specs = (
        P(("parts", "grp", "ep"), None),
        P(("parts", "grp", "ep"), None),
        P(("parts", "grp", "ep"), None),
        P(("parts", "grp", "ep"), None),
        P(("grp", "ep"), None, None),
        P(("grp", "ep"), None, None),
        P(("grp", "ep"), None, None),
    )
    out_specs = (P(("parts", "grp", "ep"), None), P(("parts", "grp", "ep"), None))
    return jax.shard_map(
        on_device, mesh=mesh, in_specs=in_specs, out_specs=out_specs, check_vma=False
    )
```

```python
import jax
import jax.numpy as jnp
from jax import lax
from jax.experimental import pallas as pl
from jax.experimental.pallas import tpu as pltpu
from jax.sharding import PartitionSpec as P

BOTH = ("grp", "ep")
LIGHT = pl.CostEstimate(flops=0, transcendentals=0, bytes_accessed=0)
ADD_COST = pl.CostEstimate(flops=10**9, transcendentals=0, bytes_accessed=0)
CONTRACT_LAST = (((1,), (1,)), ((), ()))


def expert_grads(rows_in, grads_in, w_gate, w_up, w_down):
    gate_pre = jnp.dot(rows_in, w_gate, preferred_element_type=jnp.float32)
    up_pre = jnp.dot(rows_in, w_up, preferred_element_type=jnp.float32)
    hidden_grad = lax.dot_general(grads_in, w_down, CONTRACT_LAST, preferred_element_type=jnp.float32)
    grad_gate, grad_up, weight_grad = hidden_grads(gate_pre, up_pre, hidden_grad)
    return (both_terms(grad_gate, grad_up, w_gate, w_up), weight_grad)


def both_terms(grad_gate, grad_up, w_gate, w_up):
    row_terms = lax.dot_general(grad_gate, w_gate, CONTRACT_LAST, preferred_element_type=jnp.float32)
    row_terms += lax.dot_general(grad_up, w_up, CONTRACT_LAST, preferred_element_type=jnp.float32)
    return row_terms.astype(jnp.bfloat16)


def hidden_grads(gate_pre, up_pre, hidden_grad):
    sigmoid_gate = 1.0 / (1.0 + jnp.exp(-gate_pre))
    activation = gate_pre * sigmoid_gate
    hidden = activation * up_pre
    weight_grad = jnp.sum(hidden_grad * hidden, axis=-1, keepdims=True)
    grad_up = (hidden_grad * activation).astype(jnp.bfloat16)
    grad_gate = (
        hidden_grad * up_pre * sigmoid_gate * (1.0 + gate_pre * (1.0 - sigmoid_gate))
    ).astype(jnp.bfloat16)
    return (grad_gate, grad_up, weight_grad)


def slot_plan(routes, experts, capacity):
    tok_rows, top_count = routes.shape
    flat_ids = routes.reshape(-1)
    pad_pair = flat_ids.shape[0]
    pair_ids = jnp.arange(pad_pair, dtype=jnp.int32)
    sort_order = jnp.argsort(flat_ids, stable=True)
    sorted_ids = flat_ids[sort_order]
    onehot = (flat_ids[:, None] == jnp.arange(experts, dtype=jnp.int32)[None, :]).astype(jnp.int32)
    counts = jnp.sum(onehot, axis=0)
    starts = jnp.cumsum(counts) - counts
    sorted_rank = pair_ids - starts[sorted_ids]
    sorted_slot = sorted_ids * capacity + sorted_rank
    slot_of_pair = jnp.zeros((pad_pair,), jnp.int32).at[sort_order].set(sorted_slot)
    slot_pair = jnp.full((experts * capacity,), pad_pair, jnp.int32).at[sorted_slot].set(sort_order)
    slot_token = jnp.where(slot_pair < pad_pair, slot_pair // top_count, tok_rows)
    return (slot_of_pair, slot_token)


def place_rows(source_rows, slot_token):
    padded = jnp.concatenate(
        [source_rows, jnp.zeros((1, source_rows.shape[1]), source_rows.dtype)], 0
    )
    return padded[slot_token]


def routed_plan(tokens, cotangent, expert_ids, route_weights, w_gate, w_up, w_down):
    group_count = lax.axis_size("grp")
    lane_count = lax.axis_size("ep")
    experts = group_count * lane_count
    tok_rows, top_count = expert_ids.shape
    model_width = tokens.shape[1]
    capacity = 2 * tok_rows * top_count // experts
    slot_of_pair, slot_token = slot_plan(expert_ids, experts, capacity)
    shape = (group_count, lane_count, capacity)

    def there_and(array, axes):
        for axis in axes:
            at = BOTH.index(axis)
            array = lax.all_to_all(array, axis, split_axis=at, concat_axis=at, tiled=True)
        return array

    rows_in = there_and(place_rows(tokens, slot_token).reshape(shape + (model_width,)), BOTH)
    grads_in = there_and(place_rows(cotangent, slot_token).reshape(shape + (model_width,)), BOTH)
    row_terms, weight_grad = expert_grads(
        rows_in.reshape(-1, model_width),
        grads_in.reshape(-1, model_width),
        w_gate[0],
        w_up[0],
        w_down[0],
    )
    row_terms = there_and(row_terms.reshape(shape + (model_width,)), BOTH[::-1])
    weight_grad = there_and(weight_grad.astype(jnp.bfloat16).reshape(shape), BOTH[::-1])
    row_terms = row_terms.reshape(experts * capacity, model_width)
    weight_grad = weight_grad.reshape(experts * capacity)
    picked = row_terms[slot_of_pair].reshape(tok_rows, top_count, model_width)
    grad_tokens = jnp.sum(route_weights[:, :, None] * picked.astype(jnp.float32), axis=1)
    grad_weights = weight_grad[slot_of_pair].reshape(tok_rows, top_count)
    return (grad_tokens.astype(jnp.bfloat16), grad_weights)


def after_all(*arrays):
    return lax.optimization_barrier(arrays)


def spread_experts(column, row_of, extra):
    rows = column.shape[0]
    across = lax.broadcasted_iota(jnp.int32, (rows, rows), 1)
    down = lax.broadcasted_iota(jnp.int32, (rows, rows), 0)
    line = jnp.sum(jnp.where(across == down, column, 0.0), axis=0, keepdims=True)
    return jnp.where(lax.broadcasted_iota(jnp.int32, (extra, rows), 0) == row_of, line, 0.0)


def bf16_pieces(values):
    pieces = []
    for unused in range(3):
        piece = lax.reduce_precision(values, exponent_bits=8, mantissa_bits=7)
        values = values - piece
        pieces.append(piece.astype(jnp.bfloat16))
    return pieces


def read_share(lines, expert, experts, rows):
    pieces = lines.astype(jnp.float32)
    groups = pieces.shape[1] // rows
    slot = lax.broadcasted_iota(jnp.int32, pieces.shape, 0) * groups
    slot = slot + lax.broadcasted_iota(jnp.int32, pieces.shape, 1) // rows
    wanted = (slot == expert) | (slot == expert + experts) | (slot == expert + 2 * experts)
    kept = jnp.where(wanted, pieces, 0.0)
    line = sum(kept[:, g * rows : (g + 1) * rows] for g in range(groups))
    line = jnp.sum(line, axis=0, keepdims=True)
    across = lax.broadcasted_iota(jnp.int32, (rows, rows), 1)
    down = lax.broadcasted_iota(jnp.int32, (rows, rows), 0)
    return jnp.sum(jnp.where(across == down, line, 0.0), axis=1, keepdims=True)


def hold_kernel(count, pieces, *refs):
    sources, held, sems = refs[:count], refs[count : 2 * count], refs[-1]
    copies = []
    for at in range(count):
        rows = sources[at].shape[0] // pieces
        for i in range(pieces):
            part = pl.ds(i * rows, rows)
            copies.append(pltpu.make_async_copy(sources[at].at[part], held[at].at[part], sems.at[at, i]))
    for copy in copies:
        copy.start()
    for copy in copies:
        copy.wait()


def hold(*arrays, pieces=4):
    return pl.pallas_call(
        lambda *refs: hold_kernel(len(arrays), pieces, *refs),
        in_specs=[pl.BlockSpec(memory_space=pltpu.HBM)] * len(arrays),
        out_shape=[pltpu.VMEM(array.shape, array.dtype) for array in arrays],
        scratch_shapes=[pltpu.SemaphoreType.DMA((len(arrays), pieces))],
        compiler_params=pltpu.CompilerParams(vmem_limit_bytes=24 << 20),
        cost_estimate=LIGHT,
    )(*[pltpu.with_memory_space_constraint(array, pltpu.HBM) for array in arrays])


def grads_kernel(blocks, rows, experts, extra, *refs):
    place_ref, refs = refs[0], refs[1:]
    token_refs, grad_refs, refs = refs[:blocks], refs[blocks : 2 * blocks], refs[2 * blocks :]
    weights, outs = (refs[:3], refs[3:6]), refs[6:]
    places = [jnp.max(place_ref[:, at : at + 1]) for at in range(2)]
    rows_in = jnp.concatenate([ref[...] for ref in token_refs], 0)
    with_lines = [ref[...] for ref in grad_refs]
    grads_in = jnp.concatenate([block[:rows] for block in with_lines], 0)
    total, spread = None, [None] * blocks
    for at, three in enumerate(weights):
        w_gate, w_up, w_down = (w[...] for w in three)
        gate_pre = jnp.dot(rows_in, w_gate, preferred_element_type=jnp.float32)
        up_pre = jnp.dot(rows_in, w_up, preferred_element_type=jnp.float32)
        hidden_grad = lax.dot_general(grads_in, w_down, CONTRACT_LAST, preferred_element_type=jnp.float32)
        grad_gate, grad_up, weight_grad = hidden_grads(gate_pre, up_pre, hidden_grad)
        row_terms = both_terms(grad_gate, grad_up, w_gate, w_up)
        shares = [read_share(block[rows:], places[at], experts, rows) for block in with_lines]
        scaled = jnp.concatenate(shares, 0) * row_terms.astype(jnp.float32)
        total = scaled if total is None else total + scaled
        for i in range(blocks):
            lines = spread_experts(weight_grad[i * rows : (i + 1) * rows], places[at], extra)
            spread[i] = lines if at == 0 else spread[i] + lines
    half = total.shape[1] // 2
    for i in range(blocks):
        left, right = outs[2 * i], outs[2 * i + 1]
        block = total[i * rows : (i + 1) * rows]
        left[:rows, :] = block[:, :half].astype(left.dtype)
        left[rows:, :] = jnp.zeros((extra, half), left.dtype)
        left[rows:, :rows] = spread[i].astype(jnp.bfloat16).astype(left.dtype)
        right[...] = block[:, half:].astype(right.dtype)


def block_grads(places, blocks_in, weights, experts, extra, kinds):
    tokens, grads = zip(*blocks_in)
    blocks = len(tokens)
    rows, width = tokens[0].shape
    outs = []
    for left, right in kinds:
        outs.append(jax.ShapeDtypeStruct((rows + extra, width // 2), left))
        outs.append(jax.ShapeDtypeStruct((rows, width // 2), right))
    weights = [pltpu.with_memory_space_constraint(w, pltpu.VMEM) for w in weights]
    out = pl.pallas_call(
        lambda *refs: grads_kernel(blocks, rows, experts, extra, *refs),
        out_shape=outs,
        compiler_params=pltpu.CompilerParams(vmem_limit_bytes=24 << 20),
        cost_estimate=LIGHT,
    )(places, *tokens, *grads, *weights)
    return [(out[2 * i], out[2 * i + 1]) for i in range(blocks)]


def add_kernel(*refs):
    count = len(refs) // 3
    for i in range(count):
        came, own, out = refs[2 * i], refs[2 * i + 1], refs[2 * count + i]
        out[...] = (came[...].astype(jnp.float32) + own[...]).astype(out.dtype)


def add_pairs(*pairs):
    operands = [array for pair in pairs for array in pair]
    return pl.pallas_call(
        add_kernel,
        out_shape=[jax.ShapeDtypeStruct(came.shape, came.dtype) for came, own in pairs],
        compiler_params=pltpu.CompilerParams(vmem_limit_bytes=8 << 20),
        cost_estimate=ADD_COST,
    )(*operands)


def finish_kernel(left_own, right_own, left_a, left_b, right_a, right_b, ids, tokens_out, weights_out):
    rows, half = right_own.shape
    extra = left_own.shape[0] - rows
    as_f32 = lambda ref: ref[...].astype(jnp.float32)
    left = left_own[...] + as_f32(left_a) + as_f32(left_b)
    tokens_out[:, :half] = left[:rows].astype(tokens_out.dtype)
    tokens_out[:, half:] = (right_own[...] + as_f32(right_a) + as_f32(right_b)).astype(tokens_out.dtype)
    grads = left[rows:, :rows]
    experts = lax.broadcasted_iota(jnp.int32, grads.shape, 0)
    for k in range(ids.shape[0]):
        picked = jnp.where(experts == ids[k : k + 1, :], grads, 0.0)
        weights_out[k : k + 1, :] = jnp.sum(picked, axis=0, keepdims=True).astype(weights_out.dtype)


def ring_order(chips_x, lanes):
    order = []
    for x in range(chips_x):
        column = [(x, z) for z in range(lanes)]
        order += column if x % 2 == 0 else column[::-1]
    return order


def ring_plan(tokens, cotangent, expert_ids, route_weights, w_gate, w_up, w_down):
    group_count = lax.axis_size("grp")
    lanes = lax.axis_size("ep")
    devices = group_count * lanes
    rows, width = tokens.shape
    order = ring_order(group_count // 2, lanes)
    chips = len(order)
    far = chips // 2
    extra = -(-devices // 16) * 16

    def device(place, core):
        x, z = order[place % chips]
        return (2 * x + core) * lanes + z

    ahead = [(device(p, c), device(p + 1, c)) for p in range(chips) for c in range(2)]
    behind = [(device(p, c), device(p - 1, c)) for p in range(chips) for c in range(2)]
    across = [(device(p, c), device(p, 1 - c)) for p in range(chips) for c in range(2)]

    def send(array, pairs):
        return lax.ppermute(array, BOTH, pairs)

    me = lax.axis_index("grp") * lanes + lax.axis_index("ep")
    other = jnp.where(lax.rem(lax.axis_index("grp"), 2) == 0, me + lanes, me - lanes)
    places = jnp.stack([me, other]).reshape(1, 2)

    expert_list = jnp.arange(devices, dtype=jnp.int32)
    chosen = expert_ids[None, :, :] == expert_list[:, None, None]
    dense = jnp.sum(jnp.where(chosen, route_weights[None], 0.0), axis=-1)
    lines = jnp.concatenate(bf16_pieces(dense), 0)
    line_rows = -(-3 * devices * rows // (8 * width)) * 8
    lines = jnp.pad(lines, ((0, line_rows * width // rows - 3 * devices), (0, 0))).reshape(line_rows, width)
    cotangent = jnp.concatenate([cotangent, lines], 0)
    grad_up, grad_down = send(cotangent, ahead), send(cotangent, behind)
    mine = (w_gate[0], w_up[0], w_down[0])
    other = tuple(send(w, across) for w in mine)
    second = after_all(tokens, *other)[0]
    token_up, token_down = send(second, ahead), send(second, behind)
    weights = hold(*mine, *other)

    sums = {}

    def compute(blocks):
        kinds = []
        for o, *unused in blocks:
            left = jnp.bfloat16 if o in (far, far - 1) else jnp.float32
            right = jnp.bfloat16 if o in (far, chips - far + 1) else jnp.float32
            kinds.append((left, right))
        out = block_grads(places, [(t, g) for o, t, g in blocks], weights, devices, extra, kinds)
        for (o, *unused), pair in zip(blocks, out):
            sums[o] = pair
        return out[0][0]

    arrived = [[(0, tokens, cotangent)], [(1, token_up, grad_up), (chips - 1, token_down, grad_down)]]
    for step in range(2, far):
        if step == far - 1:
            grad_up, grad_down = after_all(grad_up, grad_down, compute(arrived[0]))[:2]
        token_up, token_down = send(token_up, ahead), send(token_down, behind)
        grad_up, grad_down = send(grad_up, ahead), send(grad_down, behind)
        arrived.append([(step, token_up, grad_up), (chips - step, token_down, grad_down)])
    grad_down = after_all(grad_down, grad_up, *[compute(arrived[o]) for o in range(1, far - 2)])[0]
    token_up = after_all(token_up, token_down, compute(arrived[far - 2]))[0]
    token_up, grad_down = send(token_up, ahead), send(grad_down, behind)
    last = compute(arrived[far - 1])

    right_up, left_down = send(sums[chips - far + 1][1], ahead), send(sums[far - 1][0], behind)
    token_up = after_all(token_up, last)[0]
    compute([(far, token_up, grad_down)])
    left_up, right_down = after_all(*sums[far], right_up, left_down)[:2]
    for step in range(far, 0, -1):
        left_up, right_down = send(left_up, ahead), send(right_down, behind)
        if step > 2:
            right_up, left_down = add_pairs((right_up, sums[chips - step + 2][1]), (left_down, sums[step - 2][0]))
            right_up, left_down = send(right_up, ahead), send(left_down, behind)
        if step > 1:
            left_up, right_down = add_pairs((left_up, sums[chips - step + 1][0]), (right_down, sums[step - 1][1]))

    grad_tokens, grad_weights = pl.pallas_call(
        finish_kernel,
        out_shape=[
            jax.ShapeDtypeStruct(tokens.shape, tokens.dtype),
            jax.ShapeDtypeStruct(expert_ids.shape[::-1], jnp.bfloat16),
        ],
        compiler_params=pltpu.CompilerParams(vmem_limit_bytes=8 << 20),
        cost_estimate=LIGHT,
    )(*sums[0], left_up, left_down, right_up, right_down, expert_ids.T)
    return (grad_tokens, grad_weights.T)


def on_device(tokens, cotangent, expert_ids, route_weights, w_gate, w_up, w_down):
    group_count = lax.axis_size("grp")
    experts = group_count * lax.axis_size("ep")
    rows, top_count = expert_ids.shape
    capacity = 2 * rows * top_count // experts
    fits = rows % 128 == 0 and experts <= rows <= tokens.shape[1] // 2 and group_count % 2 == 0 and experts >= 8 and tokens.shape[1] % rows == 0
    plan = ring_plan if fits and 2 * capacity >= rows else routed_plan
    return plan(tokens, cotangent, expert_ids, route_weights, w_gate, w_up, w_down)


def solution(mesh):
    in_specs = (
        P(("parts", "grp", "ep"), None),
        P(("parts", "grp", "ep"), None),
        P(("parts", "grp", "ep"), None),
        P(("parts", "grp", "ep"), None),
        P(("grp", "ep"), None, None),
        P(("grp", "ep"), None, None),
        P(("grp", "ep"), None, None),
    )
    out_specs = (P(("parts", "grp", "ep"), None), P(("parts", "grp", "ep"), None))
    return jax.shard_map(
        on_device, mesh=mesh, in_specs=in_specs, out_specs=out_specs, check_vma=False
    )
```

```python
import jax
import jax.numpy as jnp
from jax import lax
from jax.experimental import pallas as pl
from jax.experimental.pallas import tpu as pltpu
from jax.sharding import PartitionSpec as P

BOTH = ("grp", "ep")
LIGHT = pl.CostEstimate(flops=0, transcendentals=0, bytes_accessed=0)
ADD_COST = pl.CostEstimate(flops=10**9, transcendentals=0, bytes_accessed=0)
CONTRACT_LAST = (((1,), (1,)), ((), ()))
LINES = 8


def expert_grads(rows_in, grads_in, w_gate, w_up, w_down):
    gate_pre = jnp.dot(rows_in, w_gate, preferred_element_type=jnp.float32)
    up_pre = jnp.dot(rows_in, w_up, preferred_element_type=jnp.float32)
    hidden_grad = lax.dot_general(grads_in, w_down, CONTRACT_LAST, preferred_element_type=jnp.float32)
    grad_gate, grad_up, weight_grad = hidden_grads(gate_pre, up_pre, hidden_grad)
    return (both_terms(grad_gate, grad_up, w_gate, w_up), weight_grad)


def both_terms(grad_gate, grad_up, w_gate, w_up):
    row_terms = lax.dot_general(grad_gate, w_gate, CONTRACT_LAST, preferred_element_type=jnp.float32)
    row_terms += lax.dot_general(grad_up, w_up, CONTRACT_LAST, preferred_element_type=jnp.float32)
    return row_terms.astype(jnp.bfloat16)


def hidden_grads(gate_pre, up_pre, hidden_grad):
    sigmoid_gate = 1.0 / (1.0 + jnp.exp(-gate_pre))
    activation = gate_pre * sigmoid_gate
    hidden = activation * up_pre
    weight_grad = jnp.sum(hidden_grad * hidden, axis=-1, keepdims=True)
    grad_up = (hidden_grad * activation).astype(jnp.bfloat16)
    grad_gate = (
        hidden_grad * up_pre * sigmoid_gate * (1.0 + gate_pre * (1.0 - sigmoid_gate))
    ).astype(jnp.bfloat16)
    return (grad_gate, grad_up, weight_grad)


def slot_plan(routes, experts, capacity):
    tok_rows, top_count = routes.shape
    flat_ids = routes.reshape(-1)
    pad_pair = flat_ids.shape[0]
    pair_ids = jnp.arange(pad_pair, dtype=jnp.int32)
    sort_order = jnp.argsort(flat_ids, stable=True)
    sorted_ids = flat_ids[sort_order]
    onehot = (flat_ids[:, None] == jnp.arange(experts, dtype=jnp.int32)[None, :]).astype(jnp.int32)
    counts = jnp.sum(onehot, axis=0)
    starts = jnp.cumsum(counts) - counts
    sorted_rank = pair_ids - starts[sorted_ids]
    sorted_slot = sorted_ids * capacity + sorted_rank
    slot_of_pair = jnp.zeros((pad_pair,), jnp.int32).at[sort_order].set(sorted_slot)
    slot_pair = jnp.full((experts * capacity,), pad_pair, jnp.int32).at[sorted_slot].set(sort_order)
    slot_token = jnp.where(slot_pair < pad_pair, slot_pair // top_count, tok_rows)
    return (slot_of_pair, slot_token)


def place_rows(source_rows, slot_token):
    padded = jnp.concatenate(
        [source_rows, jnp.zeros((1, source_rows.shape[1]), source_rows.dtype)], 0
    )
    return padded[slot_token]


def routed_plan(tokens, cotangent, expert_ids, route_weights, w_gate, w_up, w_down):
    group_count = lax.axis_size("grp")
    lane_count = lax.axis_size("ep")
    experts = group_count * lane_count
    tok_rows, top_count = expert_ids.shape
    model_width = tokens.shape[1]
    capacity = 2 * tok_rows * top_count // experts
    slot_of_pair, slot_token = slot_plan(expert_ids, experts, capacity)
    shape = (group_count, lane_count, capacity)

    def there_and(array, axes):
        for axis in axes:
            at = BOTH.index(axis)
            array = lax.all_to_all(array, axis, split_axis=at, concat_axis=at, tiled=True)
        return array

    rows_in = there_and(place_rows(tokens, slot_token).reshape(shape + (model_width,)), BOTH)
    grads_in = there_and(place_rows(cotangent, slot_token).reshape(shape + (model_width,)), BOTH)
    row_terms, weight_grad = expert_grads(
        rows_in.reshape(-1, model_width),
        grads_in.reshape(-1, model_width),
        w_gate[0],
        w_up[0],
        w_down[0],
    )
    row_terms = there_and(row_terms.reshape(shape + (model_width,)), BOTH[::-1])
    weight_grad = there_and(weight_grad.astype(jnp.bfloat16).reshape(shape), BOTH[::-1])
    row_terms = row_terms.reshape(experts * capacity, model_width)
    weight_grad = weight_grad.reshape(experts * capacity)
    picked = row_terms[slot_of_pair].reshape(tok_rows, top_count, model_width)
    grad_tokens = jnp.sum(route_weights[:, :, None] * picked.astype(jnp.float32), axis=1)
    grad_weights = weight_grad[slot_of_pair].reshape(tok_rows, top_count)
    return (grad_tokens.astype(jnp.bfloat16), grad_weights)


def after_all(*arrays):
    return lax.optimization_barrier(arrays)


def spread_experts(column, row_of, extra):
    rows = column.shape[0]
    across = lax.broadcasted_iota(jnp.int32, (rows, rows), 1)
    down = lax.broadcasted_iota(jnp.int32, (rows, rows), 0)
    line = jnp.sum(jnp.where(across == down, column, 0.0), axis=0, keepdims=True)
    return jnp.where(lax.broadcasted_iota(jnp.int32, (extra, rows), 0) == row_of, line, 0.0)


def lines_kernel(ids, weights, cotangent, out):
    rows, experts = cotangent.shape[0], LINES * (cotangent.shape[1] // (3 * cotangent.shape[0]))
    out[:rows, :] = cotangent[...]
    out[rows:, :] = jnp.zeros((LINES, out.shape[1]), out.dtype)
    expert = lax.broadcasted_iota(jnp.int32, (experts, rows), 0)
    left = jnp.zeros((experts, rows), jnp.float32)
    for k in range(ids.shape[0]):
        left += jnp.where(expert == ids[k : k + 1, :], weights[k : k + 1, :], 0.0)
    for piece in range(3):
        part = left.astype(jnp.bfloat16)
        left -= part.astype(jnp.float32)
        for h in range(experts // LINES):
            at = (piece * (experts // LINES) + h) * rows
            out[rows:, at : at + rows] = part[h * LINES : (h + 1) * LINES]


def with_lines(ids, weights, cotangent):
    return pl.pallas_call(
        lines_kernel,
        out_shape=jax.ShapeDtypeStruct((cotangent.shape[0] + LINES, cotangent.shape[1]), cotangent.dtype),
        compiler_params=pltpu.CompilerParams(vmem_limit_bytes=8 << 20),
        cost_estimate=LIGHT,
    )(ids.T, weights.T, cotangent)


def read_share(lines, expert, rows):
    pieces = lines.astype(jnp.float32)
    groups = pieces.shape[1] // rows
    sets = groups // 3
    group = lax.broadcasted_iota(jnp.int32, pieces.shape, 1) // rows
    line = lax.broadcasted_iota(jnp.int32, pieces.shape, 0) + LINES * (group % sets)
    kept = jnp.where((line == expert) & (group < 3 * sets), pieces, 0.0)
    line = sum(kept[:, g * rows : (g + 1) * rows] for g in range(groups))
    line = jnp.sum(line, axis=0, keepdims=True)
    across = lax.broadcasted_iota(jnp.int32, (rows, rows), 1)
    down = lax.broadcasted_iota(jnp.int32, (rows, rows), 0)
    return jnp.sum(jnp.where(across == down, line, 0.0), axis=1, keepdims=True)


def hold_kernel(count, pieces, *refs):
    sources, held, sems = refs[:count], refs[count : 2 * count], refs[-1]
    copies = []
    for at in range(count):
        rows = sources[at].shape[0] // pieces
        for i in range(pieces):
            part = pl.ds(i * rows, rows)
            copies.append(pltpu.make_async_copy(sources[at].at[part], held[at].at[part], sems.at[at, i]))
    for copy in copies:
        copy.start()
    for copy in copies:
        copy.wait()


def hold(*arrays, pieces=4):
    return pl.pallas_call(
        lambda *refs: hold_kernel(len(arrays), pieces, *refs),
        in_specs=[pl.BlockSpec(memory_space=pltpu.HBM)] * len(arrays),
        out_shape=[pltpu.VMEM(array.shape, array.dtype) for array in arrays],
        scratch_shapes=[pltpu.SemaphoreType.DMA((len(arrays), pieces))],
        compiler_params=pltpu.CompilerParams(vmem_limit_bytes=24 << 20),
        cost_estimate=LIGHT,
    )(*[pltpu.with_memory_space_constraint(array, pltpu.HBM) for array in arrays])


def grads_kernel(blocks, rows, extra, *refs):
    place_ref, refs = refs[0], refs[1:]
    token_refs, grad_refs, refs = refs[:blocks], refs[blocks : 2 * blocks], refs[2 * blocks :]
    weights, outs = (refs[:3], refs[3:6]), refs[6:]
    places = [jnp.max(place_ref[:, at : at + 1]) for at in range(2)]
    rows_in = jnp.concatenate([ref[...] for ref in token_refs], 0)
    blocks_in = [ref[...] for ref in grad_refs]
    grads_in = jnp.concatenate([block[:rows] for block in blocks_in], 0)
    total, spread = None, [None] * blocks
    for at, three in enumerate(weights):
        w_gate, w_up, w_down = (w[...] for w in three)
        gate_pre = jnp.dot(rows_in, w_gate, preferred_element_type=jnp.float32)
        up_pre = jnp.dot(rows_in, w_up, preferred_element_type=jnp.float32)
        hidden_grad = lax.dot_general(grads_in, w_down, CONTRACT_LAST, preferred_element_type=jnp.float32)
        grad_gate, grad_up, weight_grad = hidden_grads(gate_pre, up_pre, hidden_grad)
        row_terms = both_terms(grad_gate, grad_up, w_gate, w_up)
        shares = [read_share(block[rows:], places[at], rows) for block in blocks_in]
        scaled = jnp.concatenate(shares, 0) * row_terms.astype(jnp.float32)
        total = scaled if total is None else total + scaled
        for i in range(blocks):
            lines = spread_experts(weight_grad[i * rows : (i + 1) * rows], places[at], extra)
            spread[i] = lines if at == 0 else spread[i] + lines
    half = total.shape[1] // 2
    for i in range(blocks):
        left, right = outs[2 * i], outs[2 * i + 1]
        block = total[i * rows : (i + 1) * rows]
        left[:rows, :] = block[:, :half].astype(left.dtype)
        left[rows:, :] = jnp.zeros((extra, half), left.dtype)
        left[rows:, :rows] = spread[i].astype(jnp.bfloat16).astype(left.dtype)
        right[...] = block[:, half:].astype(right.dtype)


def block_grads(places, blocks_in, weights, extra, kinds):
    tokens, grads = zip(*blocks_in)
    blocks = len(tokens)
    rows, width = tokens[0].shape
    outs = []
    for left, right in kinds:
        outs.append(jax.ShapeDtypeStruct((rows + extra, width // 2), left))
        outs.append(jax.ShapeDtypeStruct((rows, width // 2), right))
    weights = [pltpu.with_memory_space_constraint(w, pltpu.VMEM) for w in weights]
    out = pl.pallas_call(
        lambda *refs: grads_kernel(blocks, rows, extra, *refs),
        out_shape=outs,
        compiler_params=pltpu.CompilerParams(vmem_limit_bytes=24 << 20),
        cost_estimate=LIGHT,
    )(places, *tokens, *grads, *weights)
    return [(out[2 * i], out[2 * i + 1]) for i in range(blocks)]


def add_kernel(*refs):
    count = len(refs) // 3
    for i in range(count):
        came, own, out = refs[2 * i], refs[2 * i + 1], refs[2 * count + i]
        out[...] = (came[...].astype(jnp.float32) + own[...]).astype(out.dtype)


def add_pairs(*pairs):
    operands = [array for pair in pairs for array in pair]
    return pl.pallas_call(
        add_kernel,
        out_shape=[jax.ShapeDtypeStruct(came.shape, came.dtype) for came, own in pairs],
        compiler_params=pltpu.CompilerParams(vmem_limit_bytes=8 << 20),
        cost_estimate=ADD_COST,
    )(*operands)


def finish_kernel(left_own, right_own, left_a, left_b, right_a, right_b, ids, tokens_out, weights_out):
    rows, half = right_own.shape
    extra = left_own.shape[0] - rows
    as_f32 = lambda ref: ref[...].astype(jnp.float32)
    left = left_own[...] + as_f32(left_a) + as_f32(left_b)
    tokens_out[:, :half] = left[:rows].astype(tokens_out.dtype)
    tokens_out[:, half:] = (right_own[...] + as_f32(right_a) + as_f32(right_b)).astype(tokens_out.dtype)
    grads = left[rows:, :rows]
    experts = lax.broadcasted_iota(jnp.int32, grads.shape, 0)
    for k in range(ids.shape[0]):
        picked = jnp.where(experts == ids[k : k + 1, :], grads, 0.0)
        weights_out[k : k + 1, :] = jnp.sum(picked, axis=0, keepdims=True).astype(weights_out.dtype)


def ring_order(chips_x, lanes):
    order = []
    for x in range(chips_x):
        column = [(x, z) for z in range(lanes)]
        order += column if x % 2 == 0 else column[::-1]
    return order


def ring_plan(tokens, cotangent, expert_ids, route_weights, w_gate, w_up, w_down):
    group_count = lax.axis_size("grp")
    lanes = lax.axis_size("ep")
    devices = group_count * lanes
    rows, width = tokens.shape
    order = ring_order(group_count // 2, lanes)
    chips = len(order)
    far = chips // 2
    extra = -(-devices // 16) * 16

    def device(place, core):
        x, z = order[place % chips]
        return (2 * x + core) * lanes + z

    ahead = [(device(p, c), device(p + 1, c)) for p in range(chips) for c in range(2)]
    behind = [(device(p, c), device(p - 1, c)) for p in range(chips) for c in range(2)]
    across = [(device(p, c), device(p, 1 - c)) for p in range(chips) for c in range(2)]

    def send(array, pairs):
        return lax.ppermute(array, BOTH, pairs)

    me = lax.axis_index("grp") * lanes + lax.axis_index("ep")
    other = jnp.where(lax.rem(lax.axis_index("grp"), 2) == 0, me + lanes, me - lanes)
    places = jnp.stack([me, other]).reshape(1, 2)

    cotangent = with_lines(expert_ids, route_weights, cotangent)
    grad_up, grad_down = send(cotangent, ahead), send(cotangent, behind)
    mine = (w_gate[0], w_up[0], w_down[0])
    other = tuple(send(w, across) for w in mine)
    second = after_all(tokens, *other[:2])[0]
    token_up, token_down = send(second, ahead), send(second, behind)
    weights = hold(*mine, *other)

    sums = {}

    def compute(blocks):
        kinds = []
        for o, *unused in blocks:
            left = jnp.bfloat16 if o in (far, far - 1) else jnp.float32
            right = jnp.bfloat16 if o in (far, chips - far + 1) else jnp.float32
            kinds.append((left, right))
        out = block_grads(places, [(t, g) for o, t, g in blocks], weights, extra, kinds)
        for (o, *unused), pair in zip(blocks, out):
            sums[o] = pair
        return out[0][0]

    arrived = [[(0, tokens, cotangent)], [(1, token_up, grad_up), (chips - 1, token_down, grad_down)]]
    for step in range(2, far):
        if step == far - 1:
            grad_up, grad_down = after_all(grad_up, grad_down, compute(arrived[0]))[:2]
        token_up, token_down = send(token_up, ahead), send(token_down, behind)
        grad_up, grad_down = send(grad_up, ahead), send(grad_down, behind)
        arrived.append([(step, token_up, grad_up), (chips - step, token_down, grad_down)])
    grad_down = after_all(grad_down, grad_up, *[compute(arrived[o]) for o in range(1, far - 2)])[0]
    token_up = after_all(token_up, compute(arrived[far - 2]))[0]
    token_up, grad_down = send(token_up, ahead), send(grad_down, behind)
    last = compute(arrived[far - 1])

    right_up, left_down = send(sums[chips - far + 1][1], ahead), send(sums[far - 1][0], behind)
    token_up = after_all(token_up, last)[0]
    compute([(far, token_up, grad_down)])
    left_up, right_down = after_all(*sums[far], right_up, left_down)[:2]
    for step in range(far, 0, -1):
        left_up, right_down = send(left_up, ahead), send(right_down, behind)
        if step > 2:
            right_up, left_down = add_pairs((right_up, sums[chips - step + 2][1]), (left_down, sums[step - 2][0]))
            right_up, left_down = send(right_up, ahead), send(left_down, behind)
        if step > 1:
            left_up, right_down = add_pairs((left_up, sums[chips - step + 1][0]), (right_down, sums[step - 1][1]))

    grad_tokens, grad_weights = pl.pallas_call(
        finish_kernel,
        out_shape=[
            jax.ShapeDtypeStruct(tokens.shape, tokens.dtype),
            jax.ShapeDtypeStruct(expert_ids.shape[::-1], jnp.bfloat16),
        ],
        compiler_params=pltpu.CompilerParams(vmem_limit_bytes=8 << 20),
        cost_estimate=LIGHT,
    )(*sums[0], left_up, left_down, right_up, right_down, expert_ids.T)
    return (grad_tokens, grad_weights.T)


def on_device(tokens, cotangent, expert_ids, route_weights, w_gate, w_up, w_down):
    group_count = lax.axis_size("grp")
    experts = group_count * lax.axis_size("ep")
    rows, top_count = expert_ids.shape
    capacity = 2 * rows * top_count // experts
    width = tokens.shape[1]
    fits = rows % 128 == 0 and width % (2 * rows) == 0 and experts <= rows
    fits = fits and experts >= 8 and experts % LINES == 0 and experts <= LINES * (width // rows // 3)
    fits = fits and group_count % 2 == 0 and 2 * capacity >= rows
    plan = ring_plan if fits else routed_plan
    return plan(tokens, cotangent, expert_ids, route_weights, w_gate, w_up, w_down)


def solution(mesh):
    in_specs = (
        P(("parts", "grp", "ep"), None),
        P(("parts", "grp", "ep"), None),
        P(("parts", "grp", "ep"), None),
        P(("parts", "grp", "ep"), None),
        P(("grp", "ep"), None, None),
        P(("grp", "ep"), None, None),
        P(("grp", "ep"), None, None),
    )
    out_specs = (P(("parts", "grp", "ep"), None), P(("parts", "grp", "ep"), None))
    return jax.shard_map(
        on_device, mesh=mesh, in_specs=in_specs, out_specs=out_specs, check_vma=False
    )
```

```python
import jax
import jax.numpy as jnp
from jax import lax
from jax.experimental import pallas as pl
from jax.experimental.pallas import tpu as pltpu
from jax.sharding import PartitionSpec as P

BOTH = ("grp", "ep")
LIGHT = pl.CostEstimate(flops=0, transcendentals=0, bytes_accessed=0)
ADD_COST = pl.CostEstimate(flops=10**9, transcendentals=0, bytes_accessed=0)
CONTRACT_LAST = (((1,), (1,)), ((), ()))
LINES = 16


def expert_grads(rows_in, grads_in, w_gate, w_up, w_down):
    gate_pre = jnp.dot(rows_in, w_gate, preferred_element_type=jnp.float32)
    up_pre = jnp.dot(rows_in, w_up, preferred_element_type=jnp.float32)
    hidden_grad = lax.dot_general(grads_in, w_down, CONTRACT_LAST, preferred_element_type=jnp.float32)
    grad_gate, grad_up, weight_grad = hidden_grads(gate_pre, up_pre, hidden_grad)
    return (both_terms(grad_gate, grad_up, w_gate, w_up), weight_grad)


def both_terms(grad_gate, grad_up, w_gate, w_up):
    row_terms = lax.dot_general(grad_gate, w_gate, CONTRACT_LAST, preferred_element_type=jnp.float32)
    row_terms += lax.dot_general(grad_up, w_up, CONTRACT_LAST, preferred_element_type=jnp.float32)
    return row_terms.astype(jnp.bfloat16)


def hidden_grads(gate_pre, up_pre, hidden_grad):
    sigmoid_gate = 1.0 / (1.0 + jnp.exp(-gate_pre))
    activation = gate_pre * sigmoid_gate
    hidden = activation * up_pre
    weight_grad = jnp.sum(hidden_grad * hidden, axis=-1, keepdims=True)
    grad_up = (hidden_grad * activation).astype(jnp.bfloat16)
    grad_gate = (
        hidden_grad * up_pre * sigmoid_gate * (1.0 + gate_pre * (1.0 - sigmoid_gate))
    ).astype(jnp.bfloat16)
    return (grad_gate, grad_up, weight_grad)


def slot_plan(routes, experts, capacity):
    tok_rows, top_count = routes.shape
    flat_ids = routes.reshape(-1)
    pad_pair = flat_ids.shape[0]
    pair_ids = jnp.arange(pad_pair, dtype=jnp.int32)
    sort_order = jnp.argsort(flat_ids, stable=True)
    sorted_ids = flat_ids[sort_order]
    onehot = (flat_ids[:, None] == jnp.arange(experts, dtype=jnp.int32)[None, :]).astype(jnp.int32)
    counts = jnp.sum(onehot, axis=0)
    starts = jnp.cumsum(counts) - counts
    sorted_rank = pair_ids - starts[sorted_ids]
    sorted_slot = sorted_ids * capacity + sorted_rank
    slot_of_pair = jnp.zeros((pad_pair,), jnp.int32).at[sort_order].set(sorted_slot)
    slot_pair = jnp.full((experts * capacity,), pad_pair, jnp.int32).at[sorted_slot].set(sort_order)
    slot_token = jnp.where(slot_pair < pad_pair, slot_pair // top_count, tok_rows)
    return (slot_of_pair, slot_token)


def place_rows(source_rows, slot_token):
    padded = jnp.concatenate(
        [source_rows, jnp.zeros((1, source_rows.shape[1]), source_rows.dtype)], 0
    )
    return padded[slot_token]


def routed_plan(tokens, cotangent, expert_ids, route_weights, w_gate, w_up, w_down):
    group_count = lax.axis_size("grp")
    lane_count = lax.axis_size("ep")
    experts = group_count * lane_count
    tok_rows, top_count = expert_ids.shape
    model_width = tokens.shape[1]
    capacity = 2 * tok_rows * top_count // experts
    slot_of_pair, slot_token = slot_plan(expert_ids, experts, capacity)
    shape = (group_count, lane_count, capacity)

    def there_and(array, axes):
        for axis in axes:
            at = BOTH.index(axis)
            array = lax.all_to_all(array, axis, split_axis=at, concat_axis=at, tiled=True)
        return array

    rows_in = there_and(place_rows(tokens, slot_token).reshape(shape + (model_width,)), BOTH)
    grads_in = there_and(place_rows(cotangent, slot_token).reshape(shape + (model_width,)), BOTH)
    row_terms, weight_grad = expert_grads(
        rows_in.reshape(-1, model_width),
        grads_in.reshape(-1, model_width),
        w_gate[0],
        w_up[0],
        w_down[0],
    )
    row_terms = there_and(row_terms.reshape(shape + (model_width,)), BOTH[::-1])
    weight_grad = there_and(weight_grad.astype(jnp.bfloat16).reshape(shape), BOTH[::-1])
    row_terms = row_terms.reshape(experts * capacity, model_width)
    weight_grad = weight_grad.reshape(experts * capacity)
    picked = row_terms[slot_of_pair].reshape(tok_rows, top_count, model_width)
    grad_tokens = jnp.sum(route_weights[:, :, None] * picked.astype(jnp.float32), axis=1)
    grad_weights = weight_grad[slot_of_pair].reshape(tok_rows, top_count)
    return (grad_tokens.astype(jnp.bfloat16), grad_weights)


def after_all(*arrays):
    return lax.optimization_barrier(arrays)


def spread_experts(column, row_of, extra):
    rows = column.shape[0]
    across = lax.broadcasted_iota(jnp.int32, (rows, rows), 1)
    down = lax.broadcasted_iota(jnp.int32, (rows, rows), 0)
    line = jnp.sum(jnp.where(across == down, column, 0.0), axis=0, keepdims=True)
    return jnp.where(lax.broadcasted_iota(jnp.int32, (extra, rows), 0) == row_of, line, 0.0)


def lines_kernel(ids, weights, cotangent, out):
    rows, experts = cotangent.shape[0], LINES * (cotangent.shape[1] // (3 * cotangent.shape[0]))
    out[:rows, :] = cotangent[...]
    out[rows:, :] = jnp.zeros((LINES, out.shape[1]), out.dtype)
    expert = lax.broadcasted_iota(jnp.int32, (experts, rows), 0)
    left = jnp.zeros((experts, rows), jnp.float32)
    for k in range(ids.shape[0]):
        left += jnp.where(expert == ids[k : k + 1, :], weights[k : k + 1, :], 0.0)
    for piece in range(3):
        part = left.astype(jnp.bfloat16)
        left -= part.astype(jnp.float32)
        for h in range(experts // LINES):
            at = (piece * (experts // LINES) + h) * rows
            out[rows:, at : at + rows] = part[h * LINES : (h + 1) * LINES]


def with_lines(ids, weights, cotangent):
    return pl.pallas_call(
        lines_kernel,
        out_shape=jax.ShapeDtypeStruct((cotangent.shape[0] + LINES, cotangent.shape[1]), cotangent.dtype),
        compiler_params=pltpu.CompilerParams(vmem_limit_bytes=8 << 20),
        cost_estimate=LIGHT,
    )(ids.T, weights.T, cotangent)


def read_share(lines, expert, rows):
    pieces = lines.astype(jnp.float32)
    groups = pieces.shape[1] // rows
    sets = groups // 3
    group = lax.broadcasted_iota(jnp.int32, pieces.shape, 1) // rows
    line = lax.broadcasted_iota(jnp.int32, pieces.shape, 0) + LINES * (group % sets)
    kept = jnp.where((line == expert) & (group < 3 * sets), pieces, 0.0)
    line = sum(kept[:, g * rows : (g + 1) * rows] for g in range(groups))
    line = jnp.sum(line, axis=0, keepdims=True)
    across = lax.broadcasted_iota(jnp.int32, (rows, rows), 1)
    down = lax.broadcasted_iota(jnp.int32, (rows, rows), 0)
    return jnp.sum(jnp.where(across == down, line, 0.0), axis=1, keepdims=True)


def hold_kernel(count, pieces, *refs):
    sources, held, sems = refs[:count], refs[count : 2 * count], refs[-1]
    copies = []
    for at in range(count):
        rows = sources[at].shape[0] // pieces
        for i in range(pieces):
            part = pl.ds(i * rows, rows)
            copies.append(pltpu.make_async_copy(sources[at].at[part], held[at].at[part], sems.at[at, i]))
    for copy in copies:
        copy.start()
    for copy in copies:
        copy.wait()


def hold(*arrays, pieces=4):
    return pl.pallas_call(
        lambda *refs: hold_kernel(len(arrays), pieces, *refs),
        in_specs=[pl.BlockSpec(memory_space=pltpu.HBM)] * len(arrays),
        out_shape=[pltpu.VMEM(array.shape, array.dtype) for array in arrays],
        scratch_shapes=[pltpu.SemaphoreType.DMA((len(arrays), pieces))],
        compiler_params=pltpu.CompilerParams(vmem_limit_bytes=24 << 20),
        cost_estimate=LIGHT,
    )(*[pltpu.with_memory_space_constraint(array, pltpu.HBM) for array in arrays])


def grads_kernel(blocks, rows, extra, *refs):
    place_ref, refs = refs[0], refs[1:]
    token_refs, grad_refs, refs = refs[:blocks], refs[blocks : 2 * blocks], refs[2 * blocks :]
    weights, outs = (refs[:3], refs[3:6]), refs[6:]
    places = [jnp.max(place_ref[:, at : at + 1]) for at in range(2)]
    rows_in = jnp.concatenate([ref[...] for ref in token_refs], 0)
    blocks_in = [ref[...] for ref in grad_refs]
    grads_in = jnp.concatenate([block[:rows] for block in blocks_in], 0)
    total, spread = None, [None] * blocks
    for at, three in enumerate(weights):
        w_gate, w_up, w_down = (w[...] for w in three)
        gate_pre = jnp.dot(rows_in, w_gate, preferred_element_type=jnp.float32)
        up_pre = jnp.dot(rows_in, w_up, preferred_element_type=jnp.float32)
        hidden_grad = lax.dot_general(grads_in, w_down, CONTRACT_LAST, preferred_element_type=jnp.float32)
        grad_gate, grad_up, weight_grad = hidden_grads(gate_pre, up_pre, hidden_grad)
        row_terms = both_terms(grad_gate, grad_up, w_gate, w_up)
        shares = [read_share(block[rows:], places[at], rows) for block in blocks_in]
        scaled = jnp.concatenate(shares, 0) * row_terms.astype(jnp.float32)
        total = scaled if total is None else total + scaled
        for i in range(blocks):
            lines = spread_experts(weight_grad[i * rows : (i + 1) * rows], places[at], extra)
            spread[i] = lines if at == 0 else spread[i] + lines
    half = total.shape[1] // 2
    for i in range(blocks):
        left, right = outs[2 * i], outs[2 * i + 1]
        block = total[i * rows : (i + 1) * rows]
        left[:rows, :] = block[:, :half].astype(left.dtype)
        left[rows:, :] = jnp.zeros((extra, half), left.dtype)
        left[rows:, :rows] = spread[i].astype(jnp.bfloat16).astype(left.dtype)
        right[...] = block[:, half:].astype(right.dtype)


def block_grads(places, blocks_in, weights, extra, kinds):
    tokens, grads = zip(*blocks_in)
    blocks = len(tokens)
    rows, width = tokens[0].shape
    outs = []
    for left, right in kinds:
        outs.append(jax.ShapeDtypeStruct((rows + extra, width // 2), left))
        outs.append(jax.ShapeDtypeStruct((rows, width // 2), right))
    weights = [pltpu.with_memory_space_constraint(w, pltpu.VMEM) for w in weights]
    out = pl.pallas_call(
        lambda *refs: grads_kernel(blocks, rows, extra, *refs),
        out_shape=outs,
        compiler_params=pltpu.CompilerParams(vmem_limit_bytes=24 << 20),
        cost_estimate=LIGHT,
    )(places, *tokens, *grads, *weights)
    return [(out[2 * i], out[2 * i + 1]) for i in range(blocks)]


def add_kernel(*refs):
    count = len(refs) // 3
    for i in range(count):
        came, own, out = refs[2 * i], refs[2 * i + 1], refs[2 * count + i]
        out[...] = (came[...].astype(jnp.float32) + own[...]).astype(out.dtype)


def add_pairs(*pairs):
    operands = [array for pair in pairs for array in pair]
    return pl.pallas_call(
        add_kernel,
        out_shape=[jax.ShapeDtypeStruct(came.shape, came.dtype) for came, own in pairs],
        compiler_params=pltpu.CompilerParams(vmem_limit_bytes=8 << 20),
        cost_estimate=ADD_COST,
    )(*operands)


def finish_kernel(left_own, right_own, left_a, left_b, right_a, right_b, ids, tokens_out, weights_out):
    rows, half = right_own.shape
    extra = left_own.shape[0] - rows
    as_f32 = lambda ref: ref[...].astype(jnp.float32)
    left = left_own[...] + as_f32(left_a) + as_f32(left_b)
    tokens_out[:, :half] = left[:rows].astype(tokens_out.dtype)
    tokens_out[:, half:] = (right_own[...] + as_f32(right_a) + as_f32(right_b)).astype(tokens_out.dtype)
    grads = left[rows:, :rows]
    experts = lax.broadcasted_iota(jnp.int32, grads.shape, 0)
    picked = [jnp.where(experts == ids[k : k + 1, :], grads, 0.0) for k in range(ids.shape[0])]
    picked = jnp.concatenate([jnp.sum(lines, axis=0, keepdims=True) for lines in picked], 0)
    weights_out[...] = picked.astype(weights_out.dtype)


def ring_order(chips_x, lanes):
    order = []
    for x in range(chips_x):
        column = [(x, z) for z in range(lanes)]
        order += column if x % 2 == 0 else column[::-1]
    return order


def ring_plan(tokens, cotangent, expert_ids, route_weights, w_gate, w_up, w_down):
    group_count = lax.axis_size("grp")
    lanes = lax.axis_size("ep")
    devices = group_count * lanes
    rows, width = tokens.shape
    order = ring_order(group_count // 2, lanes)
    chips = len(order)
    far = chips // 2
    extra = -(-devices // 16) * 16

    def device(place, core):
        x, z = order[place % chips]
        return (2 * x + core) * lanes + z

    ahead = [(device(p, c), device(p + 1, c)) for p in range(chips) for c in range(2)]
    behind = [(device(p, c), device(p - 1, c)) for p in range(chips) for c in range(2)]
    across = [(device(p, c), device(p, 1 - c)) for p in range(chips) for c in range(2)]

    def send(array, pairs):
        return lax.ppermute(array, BOTH, pairs)

    me = lax.axis_index("grp") * lanes + lax.axis_index("ep")
    other = jnp.where(lax.rem(lax.axis_index("grp"), 2) == 0, me + lanes, me - lanes)
    places = jnp.stack([me, other]).reshape(1, 2)

    cotangent = with_lines(expert_ids, route_weights, cotangent)
    grad_up, grad_down = send(cotangent, ahead), send(cotangent, behind)
    mine = (w_gate[0], w_up[0], w_down[0])
    other = tuple(send(w, across) for w in mine)
    second = after_all(tokens, *other[:2])[0]
    token_up, token_down = send(second, ahead), send(second, behind)
    weights = hold(*mine, *other)

    sums = {}

    def compute(blocks):
        kinds = []
        for o, *unused in blocks:
            left = jnp.bfloat16 if o in (far, far - 1) else jnp.float32
            right = jnp.bfloat16 if o in (far, chips - far + 1) else jnp.float32
            kinds.append((left, right))
        out = block_grads(places, [(t, g) for o, t, g in blocks], weights, extra, kinds)
        for (o, *unused), pair in zip(blocks, out):
            sums[o] = pair
        return out[0][0]

    arrived = [[(0, tokens, cotangent)], [(1, token_up, grad_up), (chips - 1, token_down, grad_down)]]
    for step in range(2, far):
        if step == far - 1:
            grad_up, grad_down = after_all(grad_up, grad_down, compute(arrived[0]))[:2]
        token_up, token_down = send(token_up, ahead), send(token_down, behind)
        grad_up, grad_down = send(grad_up, ahead), send(grad_down, behind)
        arrived.append([(step, token_up, grad_up), (chips - step, token_down, grad_down)])
    grad_down = after_all(grad_down, grad_up, *[compute(arrived[o]) for o in range(1, far - 2)])[0]
    token_up = after_all(token_up, compute(arrived[far - 2]))[0]
    token_up, grad_down = send(token_up, ahead), send(grad_down, behind)
    last = compute(arrived[far - 1])

    right_up, left_down = send(sums[chips - far + 1][1], ahead), send(sums[far - 1][0], behind)
    token_up = after_all(token_up, last)[0]
    compute([(far, token_up, grad_down)])
    left_up, right_down = after_all(*sums[far], right_up, left_down)[:2]
    for step in range(far, 0, -1):
        left_up, right_down = send(left_up, ahead), send(right_down, behind)
        if step > 2:
            right_up, left_down = add_pairs((right_up, sums[chips - step + 2][1]), (left_down, sums[step - 2][0]))
            right_up, left_down = send(right_up, ahead), send(left_down, behind)
        if step > 1:
            left_up, right_down = add_pairs((left_up, sums[chips - step + 1][0]), (right_down, sums[step - 1][1]))

    grad_tokens, grad_weights = pl.pallas_call(
        finish_kernel,
        out_shape=[
            jax.ShapeDtypeStruct(tokens.shape, tokens.dtype),
            jax.ShapeDtypeStruct(expert_ids.shape[::-1], jnp.bfloat16),
        ],
        compiler_params=pltpu.CompilerParams(vmem_limit_bytes=8 << 20),
        cost_estimate=LIGHT,
    )(*sums[0], left_up, left_down, right_up, right_down, expert_ids.T)
    return (grad_tokens, grad_weights.T)


def on_device(tokens, cotangent, expert_ids, route_weights, w_gate, w_up, w_down):
    group_count = lax.axis_size("grp")
    experts = group_count * lax.axis_size("ep")
    rows, top_count = expert_ids.shape
    capacity = 2 * rows * top_count // experts
    width = tokens.shape[1]
    fits = rows % 128 == 0 and width % (2 * rows) == 0 and experts <= rows
    fits = fits and experts >= 8 and experts % LINES == 0 and experts <= LINES * (width // rows // 3)
    fits = fits and group_count % 2 == 0 and 2 * capacity >= rows
    plan = ring_plan if fits else routed_plan
    return plan(tokens, cotangent, expert_ids, route_weights, w_gate, w_up, w_down)


def solution(mesh):
    in_specs = (
        P(("parts", "grp", "ep"), None),
        P(("parts", "grp", "ep"), None),
        P(("parts", "grp", "ep"), None),
        P(("parts", "grp", "ep"), None),
        P(("grp", "ep"), None, None),
        P(("grp", "ep"), None, None),
        P(("grp", "ep"), None, None),
    )
    out_specs = (P(("parts", "grp", "ep"), None), P(("parts", "grp", "ep"), None))
    return jax.shard_map(
        on_device, mesh=mesh, in_specs=in_specs, out_specs=out_specs, check_vma=False
    )
```

```python
import jax
import jax.numpy as jnp
from jax import lax
from jax.experimental import pallas as pl
from jax.experimental.pallas import tpu as pltpu
from jax.sharding import PartitionSpec as P

BOTH = ("grp", "ep")
LIGHT = pl.CostEstimate(flops=0, transcendentals=0, bytes_accessed=0)
ADD_COST = pl.CostEstimate(flops=10**9, transcendentals=0, bytes_accessed=0)
CONTRACT_LAST = (((1,), (1,)), ((), ()))
LINES = 8


def expert_grads(rows_in, grads_in, w_gate, w_up, w_down):
    gate_pre = jnp.dot(rows_in, w_gate, preferred_element_type=jnp.float32)
    up_pre = jnp.dot(rows_in, w_up, preferred_element_type=jnp.float32)
    hidden_grad = lax.dot_general(grads_in, w_down, CONTRACT_LAST, preferred_element_type=jnp.float32)
    grad_gate, grad_up, weight_grad = hidden_grads(gate_pre, up_pre, hidden_grad)
    return (both_terms(grad_gate, grad_up, w_gate, w_up), weight_grad)


def both_terms(grad_gate, grad_up, w_gate, w_up):
    row_terms = lax.dot_general(grad_gate, w_gate, CONTRACT_LAST, preferred_element_type=jnp.float32)
    row_terms += lax.dot_general(grad_up, w_up, CONTRACT_LAST, preferred_element_type=jnp.float32)
    return row_terms.astype(jnp.bfloat16)


def hidden_grads(gate_pre, up_pre, hidden_grad):
    sigmoid_gate = 1.0 / (1.0 + jnp.exp(-gate_pre))
    activation = gate_pre * sigmoid_gate
    hidden = activation * up_pre
    weight_grad = jnp.sum(hidden_grad * hidden, axis=-1, keepdims=True)
    grad_up = (hidden_grad * activation).astype(jnp.bfloat16)
    grad_gate = (
        hidden_grad * up_pre * sigmoid_gate * (1.0 + gate_pre * (1.0 - sigmoid_gate))
    ).astype(jnp.bfloat16)
    return (grad_gate, grad_up, weight_grad)


def slot_plan(routes, experts, capacity):
    tok_rows, top_count = routes.shape
    flat_ids = routes.reshape(-1)
    pad_pair = flat_ids.shape[0]
    pair_ids = jnp.arange(pad_pair, dtype=jnp.int32)
    sort_order = jnp.argsort(flat_ids, stable=True)
    sorted_ids = flat_ids[sort_order]
    onehot = (flat_ids[:, None] == jnp.arange(experts, dtype=jnp.int32)[None, :]).astype(jnp.int32)
    counts = jnp.sum(onehot, axis=0)
    starts = jnp.cumsum(counts) - counts
    sorted_rank = pair_ids - starts[sorted_ids]
    sorted_slot = sorted_ids * capacity + sorted_rank
    slot_of_pair = jnp.zeros((pad_pair,), jnp.int32).at[sort_order].set(sorted_slot)
    slot_pair = jnp.full((experts * capacity,), pad_pair, jnp.int32).at[sorted_slot].set(sort_order)
    slot_token = jnp.where(slot_pair < pad_pair, slot_pair // top_count, tok_rows)
    return (slot_of_pair, slot_token)


def place_rows(source_rows, slot_token):
    padded = jnp.concatenate(
        [source_rows, jnp.zeros((1, source_rows.shape[1]), source_rows.dtype)], 0
    )
    return padded[slot_token]


def routed_plan(tokens, cotangent, expert_ids, route_weights, w_gate, w_up, w_down):
    group_count = lax.axis_size("grp")
    lane_count = lax.axis_size("ep")
    experts = group_count * lane_count
    tok_rows, top_count = expert_ids.shape
    model_width = tokens.shape[1]
    capacity = 2 * tok_rows * top_count // experts
    slot_of_pair, slot_token = slot_plan(expert_ids, experts, capacity)
    shape = (group_count, lane_count, capacity)

    def there_and(array, axes):
        for axis in axes:
            at = BOTH.index(axis)
            array = lax.all_to_all(array, axis, split_axis=at, concat_axis=at, tiled=True)
        return array

    rows_in = there_and(place_rows(tokens, slot_token).reshape(shape + (model_width,)), BOTH)
    grads_in = there_and(place_rows(cotangent, slot_token).reshape(shape + (model_width,)), BOTH)
    row_terms, weight_grad = expert_grads(
        rows_in.reshape(-1, model_width),
        grads_in.reshape(-1, model_width),
        w_gate[0],
        w_up[0],
        w_down[0],
    )
    row_terms = there_and(row_terms.reshape(shape + (model_width,)), BOTH[::-1])
    weight_grad = there_and(weight_grad.astype(jnp.bfloat16).reshape(shape), BOTH[::-1])
    row_terms = row_terms.reshape(experts * capacity, model_width)
    weight_grad = weight_grad.reshape(experts * capacity)
    picked = row_terms[slot_of_pair].reshape(tok_rows, top_count, model_width)
    grad_tokens = jnp.sum(route_weights[:, :, None] * picked.astype(jnp.float32), axis=1)
    grad_weights = weight_grad[slot_of_pair].reshape(tok_rows, top_count)
    return (grad_tokens.astype(jnp.bfloat16), grad_weights)


def after_all(*arrays):
    return lax.optimization_barrier(arrays)


def spread_experts(column, row_of, extra):
    rows = column.shape[0]
    across = lax.broadcasted_iota(jnp.int32, (rows, rows), 1)
    down = lax.broadcasted_iota(jnp.int32, (rows, rows), 0)
    line = jnp.sum(jnp.where(across == down, column, 0.0), axis=0, keepdims=True)
    return jnp.where(lax.broadcasted_iota(jnp.int32, (extra, rows), 0) == row_of, line, 0.0)


def lines_kernel(ids, weights, cotangent, out):
    rows, experts = cotangent.shape[0], LINES * (cotangent.shape[1] // (3 * cotangent.shape[0]))
    expert = lax.broadcasted_iota(jnp.int32, (experts, rows), 0)
    left = jnp.zeros((experts, rows), jnp.float32)
    for k in range(ids.shape[0]):
        left += jnp.where(expert == ids[k : k + 1, :], weights[k : k + 1, :], 0.0)
    parts = []
    for unused in range(3):
        part = left.astype(jnp.bfloat16).astype(jnp.float32)
        left -= part
        parts += [part[at : at + LINES] for at in range(0, experts, LINES)]
    room = out.shape[1] - len(parts) * rows
    lines = jnp.concatenate(parts + [jnp.zeros((LINES, room), jnp.float32)] * (room > 0), 1)
    out[...] = jnp.concatenate([cotangent[...], lines.astype(out.dtype)], 0)


def with_lines(ids, weights, cotangent):
    return pl.pallas_call(
        lines_kernel,
        out_shape=jax.ShapeDtypeStruct((cotangent.shape[0] + LINES, cotangent.shape[1]), cotangent.dtype),
        compiler_params=pltpu.CompilerParams(vmem_limit_bytes=8 << 20),
        cost_estimate=LIGHT,
    )(ids.T, weights.T, cotangent)


def read_share(lines, expert, rows):
    pieces = lines.astype(jnp.float32)
    groups = pieces.shape[1] // rows
    sets = groups // 3
    group = lax.broadcasted_iota(jnp.int32, pieces.shape, 1) // rows
    line = lax.broadcasted_iota(jnp.int32, pieces.shape, 0) + LINES * (group % sets)
    kept = jnp.where((line == expert) & (group < 3 * sets), pieces, 0.0)
    line = sum(kept[:, g * rows : (g + 1) * rows] for g in range(groups))
    line = jnp.sum(line, axis=0, keepdims=True)
    across = lax.broadcasted_iota(jnp.int32, (rows, rows), 1)
    down = lax.broadcasted_iota(jnp.int32, (rows, rows), 0)
    return jnp.sum(jnp.where(across == down, line, 0.0), axis=1, keepdims=True)


def hold_kernel(count, pieces, *refs):
    sources, held, sems = refs[:count], refs[count : 2 * count], refs[-1]
    copies = []
    for at in range(count):
        rows = sources[at].shape[0] // pieces
        for i in range(pieces):
            part = pl.ds(i * rows, rows)
            copies.append(pltpu.make_async_copy(sources[at].at[part], held[at].at[part], sems.at[at, i]))
    for copy in copies:
        copy.start()
    for copy in copies:
        copy.wait()


def hold(*arrays, pieces=4):
    return pl.pallas_call(
        lambda *refs: hold_kernel(len(arrays), pieces, *refs),
        in_specs=[pl.BlockSpec(memory_space=pltpu.HBM)] * len(arrays),
        out_shape=[pltpu.VMEM(array.shape, array.dtype) for array in arrays],
        scratch_shapes=[pltpu.SemaphoreType.DMA((len(arrays), pieces))],
        compiler_params=pltpu.CompilerParams(vmem_limit_bytes=24 << 20),
        cost_estimate=LIGHT,
    )(*[pltpu.with_memory_space_constraint(array, pltpu.HBM) for array in arrays])


def grads_kernel(blocks, rows, extra, *refs):
    place_ref, refs = refs[0], refs[1:]
    token_refs, grad_refs, refs = refs[:blocks], refs[blocks : 2 * blocks], refs[2 * blocks :]
    weights, outs = (refs[:3], refs[3:6]), refs[6:]
    places = [jnp.max(place_ref[:, at : at + 1]) for at in range(2)]
    rows_in = jnp.concatenate([ref[...] for ref in token_refs], 0)
    blocks_in = [ref[...] for ref in grad_refs]
    grads_in = jnp.concatenate([block[:rows] for block in blocks_in], 0)
    total, spread = None, [None] * blocks
    for at, three in enumerate(weights):
        w_gate, w_up, w_down = (w[...] for w in three)
        gate_pre = jnp.dot(rows_in, w_gate, preferred_element_type=jnp.float32)
        up_pre = jnp.dot(rows_in, w_up, preferred_element_type=jnp.float32)
        hidden_grad = lax.dot_general(grads_in, w_down, CONTRACT_LAST, preferred_element_type=jnp.float32)
        grad_gate, grad_up, weight_grad = hidden_grads(gate_pre, up_pre, hidden_grad)
        row_terms = both_terms(grad_gate, grad_up, w_gate, w_up)
        shares = [read_share(block[rows:], places[at], rows) for block in blocks_in]
        scaled = jnp.concatenate(shares, 0) * row_terms.astype(jnp.float32)
        total = scaled if total is None else total + scaled
        for i in range(blocks):
            lines = spread_experts(weight_grad[i * rows : (i + 1) * rows], places[at], extra)
            spread[i] = lines if at == 0 else spread[i] + lines
    half = total.shape[1] // 2
    for i in range(blocks):
        left, right = outs[2 * i], outs[2 * i + 1]
        block = total[i * rows : (i + 1) * rows]
        left[:rows, :] = block[:, :half].astype(left.dtype)
        left[rows:, :] = jnp.zeros((extra, half), left.dtype)
        left[rows:, :rows] = spread[i].astype(jnp.bfloat16).astype(left.dtype)
        right[...] = block[:, half:].astype(right.dtype)


def block_grads(places, blocks_in, weights, extra, kinds):
    tokens, grads = zip(*blocks_in)
    blocks = len(tokens)
    rows, width = tokens[0].shape
    outs = []
    for left, right in kinds:
        outs.append(jax.ShapeDtypeStruct((rows + extra, width // 2), left))
        outs.append(jax.ShapeDtypeStruct((rows, width // 2), right))
    weights = [pltpu.with_memory_space_constraint(w, pltpu.VMEM) for w in weights]
    out = pl.pallas_call(
        lambda *refs: grads_kernel(blocks, rows, extra, *refs),
        out_shape=outs,
        compiler_params=pltpu.CompilerParams(vmem_limit_bytes=24 << 20),
        cost_estimate=LIGHT,
    )(places, *tokens, *grads, *weights)
    return [(out[2 * i], out[2 * i + 1]) for i in range(blocks)]


def add_kernel(*refs):
    count = len(refs) // 3
    for i in range(count):
        came, own, out = refs[2 * i], refs[2 * i + 1], refs[2 * count + i]
        out[...] = (came[...].astype(jnp.float32) + own[...]).astype(out.dtype)


def add_pairs(*pairs):
    operands = [array for pair in pairs for array in pair]
    return pl.pallas_call(
        add_kernel,
        out_shape=[jax.ShapeDtypeStruct(came.shape, came.dtype) for came, own in pairs],
        compiler_params=pltpu.CompilerParams(vmem_limit_bytes=8 << 20),
        cost_estimate=ADD_COST,
    )(*operands)


def finish_kernel(left_own, right_own, left_a, left_b, right_a, right_b, ids, tokens_out, weights_out):
    rows, half = right_own.shape
    extra = left_own.shape[0] - rows
    as_f32 = lambda ref: ref[...].astype(jnp.float32)
    left = left_own[...] + as_f32(left_a) + as_f32(left_b)
    tokens_out[:, :half] = left[:rows].astype(tokens_out.dtype)
    tokens_out[:, half:] = (right_own[...] + as_f32(right_a) + as_f32(right_b)).astype(tokens_out.dtype)
    grads = left[rows:, :rows]
    experts = lax.broadcasted_iota(jnp.int32, grads.shape, 0)
    picked = [jnp.where(experts == ids[k : k + 1, :], grads, 0.0) for k in range(ids.shape[0])]
    picked = jnp.concatenate([jnp.sum(lines, axis=0, keepdims=True) for lines in picked], 0)
    weights_out[...] = picked.astype(weights_out.dtype)


def ring_order(chips_x, lanes):
    order = []
    for x in range(chips_x):
        column = [(x, z) for z in range(lanes)]
        order += column if x % 2 == 0 else column[::-1]
    return order


def ring_plan(tokens, cotangent, expert_ids, route_weights, w_gate, w_up, w_down):
    group_count = lax.axis_size("grp")
    lanes = lax.axis_size("ep")
    devices = group_count * lanes
    rows, width = tokens.shape
    order = ring_order(group_count // 2, lanes)
    chips = len(order)
    far = chips // 2
    extra = -(-devices // 16) * 16

    def device(place, core):
        x, z = order[place % chips]
        return (2 * x + core) * lanes + z

    ahead = [(device(p, c), device(p + 1, c)) for p in range(chips) for c in range(2)]
    behind = [(device(p, c), device(p - 1, c)) for p in range(chips) for c in range(2)]
    across = [(device(p, c), device(p, 1 - c)) for p in range(chips) for c in range(2)]

    def send(array, pairs):
        return lax.ppermute(array, BOTH, pairs)

    me = lax.axis_index("grp") * lanes + lax.axis_index("ep")
    other = jnp.where(lax.rem(lax.axis_index("grp"), 2) == 0, me + lanes, me - lanes)
    places = jnp.stack([me, other]).reshape(1, 2)

    cotangent = with_lines(expert_ids, route_weights, cotangent)
    grad_up, grad_down = send(cotangent, ahead), send(cotangent, behind)
    mine = (w_gate[0], w_up[0], w_down[0])
    other = tuple(send(w, across) for w in mine)
    second = after_all(tokens, *other[:2])[0]
    token_up, token_down = send(second, ahead), send(second, behind)
    weights = hold(*mine, *other)

    sums = {}

    def compute(blocks):
        kinds = []
        for o, *unused in blocks:
            left = jnp.bfloat16 if o in (far, far - 1) else jnp.float32
            right = jnp.bfloat16 if o in (far, chips - far + 1) else jnp.float32
            kinds.append((left, right))
        out = block_grads(places, [(t, g) for o, t, g in blocks], weights, extra, kinds)
        for (o, *unused), pair in zip(blocks, out):
            sums[o] = pair
        return out[0][0]

    arrived = [[(0, tokens, cotangent)], [(1, token_up, grad_up), (chips - 1, token_down, grad_down)]]
    for step in range(2, far):
        if step == far - 1:
            grad_up, grad_down = after_all(grad_up, grad_down, compute(arrived[0]))[:2]
        token_up, token_down = send(token_up, ahead), send(token_down, behind)
        grad_up, grad_down = send(grad_up, ahead), send(grad_down, behind)
        arrived.append([(step, token_up, grad_up), (chips - step, token_down, grad_down)])
    grad_down = after_all(grad_down, grad_up, *[compute(arrived[o]) for o in range(1, far - 2)])[0]
    token_up = after_all(token_up, compute(arrived[far - 2]))[0]
    token_up, grad_down = send(token_up, ahead), send(grad_down, behind)
    last = compute(arrived[far - 1])

    right_up, left_down = send(sums[chips - far + 1][1], ahead), send(sums[far - 1][0], behind)
    token_up = after_all(token_up, last)[0]
    compute([(far, token_up, grad_down)])
    left_up, right_down = after_all(*sums[far], right_up, left_down)[:2]
    for step in range(far, 0, -1):
        left_up, right_down = send(left_up, ahead), send(right_down, behind)
        if step > 2:
            right_up, left_down = add_pairs((right_up, sums[chips - step + 2][1]), (left_down, sums[step - 2][0]))
            right_up, left_down = send(right_up, ahead), send(left_down, behind)
        if step > 1:
            left_up, right_down = add_pairs((left_up, sums[chips - step + 1][0]), (right_down, sums[step - 1][1]))

    grad_tokens, grad_weights = pl.pallas_call(
        finish_kernel,
        out_shape=[
            jax.ShapeDtypeStruct(tokens.shape, tokens.dtype),
            jax.ShapeDtypeStruct(expert_ids.shape[::-1], jnp.bfloat16),
        ],
        compiler_params=pltpu.CompilerParams(vmem_limit_bytes=8 << 20),
        cost_estimate=LIGHT,
    )(*sums[0], left_up, left_down, right_up, right_down, expert_ids.T)
    return (grad_tokens, grad_weights.T)


def on_device(tokens, cotangent, expert_ids, route_weights, w_gate, w_up, w_down):
    group_count = lax.axis_size("grp")
    experts = group_count * lax.axis_size("ep")
    rows, top_count = expert_ids.shape
    capacity = 2 * rows * top_count // experts
    width = tokens.shape[1]
    fits = rows % 128 == 0 and width % (2 * rows) == 0 and experts <= rows
    fits = fits and experts >= 8 and experts % LINES == 0 and experts <= LINES * (width // rows // 3)
    fits = fits and group_count % 2 == 0 and 2 * capacity >= rows
    plan = ring_plan if fits else routed_plan
    return plan(tokens, cotangent, expert_ids, route_weights, w_gate, w_up, w_down)


def solution(mesh):
    in_specs = (
        P(("parts", "grp", "ep"), None),
        P(("parts", "grp", "ep"), None),
        P(("parts", "grp", "ep"), None),
        P(("parts", "grp", "ep"), None),
        P(("grp", "ep"), None, None),
        P(("grp", "ep"), None, None),
        P(("grp", "ep"), None, None),
    )
    out_specs = (P(("parts", "grp", "ep"), None), P(("parts", "grp", "ep"), None))
    return jax.shard_map(
        on_device, mesh=mesh, in_specs=in_specs, out_specs=out_specs, check_vma=False
    )
```

```python
import jax
import jax.numpy as jnp
from jax import lax
from jax.experimental import pallas as pl
from jax.experimental.pallas import tpu as pltpu
from jax.sharding import PartitionSpec as P

BOTH = ("grp", "ep")
LIGHT = pl.CostEstimate(flops=0, transcendentals=0, bytes_accessed=0)
ADD_COST = pl.CostEstimate(flops=10**9, transcendentals=0, bytes_accessed=0)
CONTRACT_LAST = (((1,), (1,)), ((), ()))
LINES = 8


def expert_grads(rows_in, grads_in, w_gate, w_up, w_down):
    gate_pre = jnp.dot(rows_in, w_gate, preferred_element_type=jnp.float32)
    up_pre = jnp.dot(rows_in, w_up, preferred_element_type=jnp.float32)
    hidden_grad = lax.dot_general(grads_in, w_down, CONTRACT_LAST, preferred_element_type=jnp.float32)
    grad_gate, grad_up, weight_grad = hidden_grads(gate_pre, up_pre, hidden_grad)
    return (both_terms(grad_gate, grad_up, w_gate, w_up), weight_grad)


def both_terms(grad_gate, grad_up, w_gate, w_up):
    row_terms = lax.dot_general(grad_gate, w_gate, CONTRACT_LAST, preferred_element_type=jnp.float32)
    row_terms += lax.dot_general(grad_up, w_up, CONTRACT_LAST, preferred_element_type=jnp.float32)
    return row_terms.astype(jnp.bfloat16)


def hidden_grads(gate_pre, up_pre, hidden_grad):
    sigmoid_gate = 1.0 / (1.0 + jnp.exp(-gate_pre))
    activation = gate_pre * sigmoid_gate
    hidden = activation * up_pre
    weight_grad = jnp.sum(hidden_grad * hidden, axis=-1, keepdims=True)
    grad_up = (hidden_grad * activation).astype(jnp.bfloat16)
    grad_gate = (
        hidden_grad * up_pre * sigmoid_gate * (1.0 + gate_pre * (1.0 - sigmoid_gate))
    ).astype(jnp.bfloat16)
    return (grad_gate, grad_up, weight_grad)


def slot_plan(routes, experts, capacity):
    tok_rows, top_count = routes.shape
    flat_ids = routes.reshape(-1)
    pad_pair = flat_ids.shape[0]
    pair_ids = jnp.arange(pad_pair, dtype=jnp.int32)
    sort_order = jnp.argsort(flat_ids, stable=True)
    sorted_ids = flat_ids[sort_order]
    onehot = (flat_ids[:, None] == jnp.arange(experts, dtype=jnp.int32)[None, :]).astype(jnp.int32)
    counts = jnp.sum(onehot, axis=0)
    starts = jnp.cumsum(counts) - counts
    sorted_rank = pair_ids - starts[sorted_ids]
    sorted_slot = sorted_ids * capacity + sorted_rank
    slot_of_pair = jnp.zeros((pad_pair,), jnp.int32).at[sort_order].set(sorted_slot)
    slot_pair = jnp.full((experts * capacity,), pad_pair, jnp.int32).at[sorted_slot].set(sort_order)
    slot_token = jnp.where(slot_pair < pad_pair, slot_pair // top_count, tok_rows)
    return (slot_of_pair, slot_token)


def place_rows(source_rows, slot_token):
    padded = jnp.concatenate(
        [source_rows, jnp.zeros((1, source_rows.shape[1]), source_rows.dtype)], 0
    )
    return padded[slot_token]


def routed_plan(tokens, cotangent, expert_ids, route_weights, w_gate, w_up, w_down):
    group_count = lax.axis_size("grp")
    lane_count = lax.axis_size("ep")
    experts = group_count * lane_count
    tok_rows, top_count = expert_ids.shape
    model_width = tokens.shape[1]
    capacity = 2 * tok_rows * top_count // experts
    slot_of_pair, slot_token = slot_plan(expert_ids, experts, capacity)
    shape = (group_count, lane_count, capacity)

    def there_and(array, axes):
        for axis in axes:
            at = BOTH.index(axis)
            array = lax.all_to_all(array, axis, split_axis=at, concat_axis=at, tiled=True)
        return array

    rows_in = there_and(place_rows(tokens, slot_token).reshape(shape + (model_width,)), BOTH)
    grads_in = there_and(place_rows(cotangent, slot_token).reshape(shape + (model_width,)), BOTH)
    row_terms, weight_grad = expert_grads(
        rows_in.reshape(-1, model_width),
        grads_in.reshape(-1, model_width),
        w_gate[0],
        w_up[0],
        w_down[0],
    )
    row_terms = there_and(row_terms.reshape(shape + (model_width,)), BOTH[::-1])
    weight_grad = there_and(weight_grad.astype(jnp.bfloat16).reshape(shape), BOTH[::-1])
    row_terms = row_terms.reshape(experts * capacity, model_width)
    weight_grad = weight_grad.reshape(experts * capacity)
    picked = row_terms[slot_of_pair].reshape(tok_rows, top_count, model_width)
    grad_tokens = jnp.sum(route_weights[:, :, None] * picked.astype(jnp.float32), axis=1)
    grad_weights = weight_grad[slot_of_pair].reshape(tok_rows, top_count)
    return (grad_tokens.astype(jnp.bfloat16), grad_weights)


def after_all(*arrays):
    return lax.optimization_barrier(arrays)


def spread_experts(column, row_of, extra):
    rows = column.shape[0]
    across = lax.broadcasted_iota(jnp.int32, (rows, rows), 1)
    down = lax.broadcasted_iota(jnp.int32, (rows, rows), 0)
    line = jnp.sum(jnp.where(across == down, column, 0.0), axis=0, keepdims=True)
    return jnp.where(lax.broadcasted_iota(jnp.int32, (extra, rows), 0) == row_of, line, 0.0)


def lines_kernel(ids, weights, cotangent, out):
    rows, experts = cotangent.shape[0], LINES * (cotangent.shape[1] // (3 * cotangent.shape[0]))
    expert = lax.broadcasted_iota(jnp.int32, (experts, rows), 0)
    left = jnp.zeros((experts, rows), jnp.float32)
    for k in range(ids.shape[0]):
        left += jnp.where(expert == ids[k : k + 1, :], weights[k : k + 1, :], 0.0)
    parts = []
    for unused in range(3):
        part = left.astype(jnp.bfloat16).astype(jnp.float32)
        left -= part
        parts += [part[at : at + LINES] for at in range(0, experts, LINES)]
    room = out.shape[1] - len(parts) * rows
    lines = jnp.concatenate(parts + [jnp.zeros((LINES, room), jnp.float32)] * (room > 0), 1)
    out[...] = jnp.concatenate([cotangent[...], lines.astype(out.dtype)], 0)


def with_lines(ids, weights, cotangent):
    return pl.pallas_call(
        lines_kernel,
        out_shape=jax.ShapeDtypeStruct((cotangent.shape[0] + LINES, cotangent.shape[1]), cotangent.dtype),
        compiler_params=pltpu.CompilerParams(vmem_limit_bytes=8 << 20),
        cost_estimate=LIGHT,
    )(ids.T, weights.T, cotangent)


def read_share(lines, expert, rows):
    pieces = lines.astype(jnp.float32)
    groups = pieces.shape[1] // rows
    sets = groups // 3
    group = lax.broadcasted_iota(jnp.int32, pieces.shape, 1) // rows
    line = lax.broadcasted_iota(jnp.int32, pieces.shape, 0) + LINES * (group % sets)
    kept = jnp.where((line == expert) & (group < 3 * sets), pieces, 0.0)
    line = sum(kept[:, g * rows : (g + 1) * rows] for g in range(groups))
    line = jnp.sum(line, axis=0, keepdims=True)
    across = lax.broadcasted_iota(jnp.int32, (rows, rows), 1)
    down = lax.broadcasted_iota(jnp.int32, (rows, rows), 0)
    return jnp.sum(jnp.where(across == down, line, 0.0), axis=1, keepdims=True)


def hold_kernel(count, pieces, *refs):
    sources, held, sems = refs[:count], refs[count : 2 * count], refs[-1]
    copies = []
    for at in range(count):
        rows = sources[at].shape[0] // pieces
        for i in range(pieces):
            part = pl.ds(i * rows, rows)
            copies.append(pltpu.make_async_copy(sources[at].at[part], held[at].at[part], sems.at[at, i]))
    for copy in copies:
        copy.start()
    for copy in copies:
        copy.wait()


def hold(*arrays, pieces=8):
    return pl.pallas_call(
        lambda *refs: hold_kernel(len(arrays), pieces, *refs),
        in_specs=[pl.BlockSpec(memory_space=pltpu.HBM)] * len(arrays),
        out_shape=[pltpu.VMEM(array.shape, array.dtype) for array in arrays],
        scratch_shapes=[pltpu.SemaphoreType.DMA((len(arrays), pieces))],
        compiler_params=pltpu.CompilerParams(vmem_limit_bytes=24 << 20),
        cost_estimate=LIGHT,
    )(*[pltpu.with_memory_space_constraint(array, pltpu.HBM) for array in arrays])


def grads_kernel(blocks, rows, extra, *refs):
    place_ref, refs = refs[0], refs[1:]
    token_refs, grad_refs, refs = refs[:blocks], refs[blocks : 2 * blocks], refs[2 * blocks :]
    weights, outs = (refs[:3], refs[3:6]), refs[6:]
    places = [jnp.max(place_ref[:, at : at + 1]) for at in range(2)]
    rows_in = jnp.concatenate([ref[...] for ref in token_refs], 0)
    blocks_in = [ref[...] for ref in grad_refs]
    grads_in = jnp.concatenate([block[:rows] for block in blocks_in], 0)
    total, spread = None, [None] * blocks
    for at, three in enumerate(weights):
        w_gate, w_up, w_down = (w[...] for w in three)
        gate_pre = jnp.dot(rows_in, w_gate, preferred_element_type=jnp.float32)
        up_pre = jnp.dot(rows_in, w_up, preferred_element_type=jnp.float32)
        hidden_grad = lax.dot_general(grads_in, w_down, CONTRACT_LAST, preferred_element_type=jnp.float32)
        grad_gate, grad_up, weight_grad = hidden_grads(gate_pre, up_pre, hidden_grad)
        row_terms = both_terms(grad_gate, grad_up, w_gate, w_up)
        shares = [read_share(block[rows:], places[at], rows) for block in blocks_in]
        scaled = jnp.concatenate(shares, 0) * row_terms.astype(jnp.float32)
        total = scaled if total is None else total + scaled
        for i in range(blocks):
            lines = spread_experts(weight_grad[i * rows : (i + 1) * rows], places[at], extra)
            spread[i] = lines if at == 0 else spread[i] + lines
    half = total.shape[1] // 2
    for i in range(blocks):
        left, right = outs[2 * i], outs[2 * i + 1]
        block = total[i * rows : (i + 1) * rows]
        left[:rows, :] = block[:, :half].astype(left.dtype)
        left[rows:, :] = jnp.zeros((extra, half), left.dtype)
        left[rows:, :rows] = spread[i].astype(jnp.bfloat16).astype(left.dtype)
        right[...] = block[:, half:].astype(right.dtype)


def block_grads(places, blocks_in, weights, extra, kinds):
    tokens, grads = zip(*blocks_in)
    blocks = len(tokens)
    rows, width = tokens[0].shape
    outs = []
    for left, right in kinds:
        outs.append(jax.ShapeDtypeStruct((rows + extra, width // 2), left))
        outs.append(jax.ShapeDtypeStruct((rows, width // 2), right))
    weights = [pltpu.with_memory_space_constraint(w, pltpu.VMEM) for w in weights]
    out = pl.pallas_call(
        lambda *refs: grads_kernel(blocks, rows, extra, *refs),
        out_shape=outs,
        compiler_params=pltpu.CompilerParams(vmem_limit_bytes=24 << 20),
        cost_estimate=LIGHT,
    )(places, *tokens, *grads, *weights)
    return [(out[2 * i], out[2 * i + 1]) for i in range(blocks)]


def add_kernel(*refs):
    count = len(refs) // 3
    for i in range(count):
        came, own, out = refs[2 * i], refs[2 * i + 1], refs[2 * count + i]
        out[...] = (came[...].astype(jnp.float32) + own[...]).astype(out.dtype)


def add_pairs(*pairs):
    operands = [array for pair in pairs for array in pair]
    return pl.pallas_call(
        add_kernel,
        out_shape=[jax.ShapeDtypeStruct(came.shape, came.dtype) for came, own in pairs],
        compiler_params=pltpu.CompilerParams(vmem_limit_bytes=8 << 20),
        cost_estimate=ADD_COST,
    )(*operands)


def finish_kernel(left_own, right_own, left_a, left_b, right_a, right_b, ids, tokens_out, weights_out):
    rows, half = right_own.shape
    extra = left_own.shape[0] - rows
    as_f32 = lambda ref: ref[...].astype(jnp.float32)
    left = left_own[...] + as_f32(left_a) + as_f32(left_b)
    tokens_out[:, :half] = left[:rows].astype(tokens_out.dtype)
    tokens_out[:, half:] = (right_own[...] + as_f32(right_a) + as_f32(right_b)).astype(tokens_out.dtype)
    grads = left[rows:, :rows]
    experts = lax.broadcasted_iota(jnp.int32, grads.shape, 0)
    picked = [jnp.where(experts == ids[k : k + 1, :], grads, 0.0) for k in range(ids.shape[0])]
    picked = jnp.concatenate([jnp.sum(lines, axis=0, keepdims=True) for lines in picked], 0)
    weights_out[...] = picked.astype(weights_out.dtype)


def ring_order(chips_x, lanes):
    order = []
    for x in range(chips_x):
        column = [(x, z) for z in range(lanes)]
        order += column if x % 2 == 0 else column[::-1]
    return order


def ring_plan(tokens, cotangent, expert_ids, route_weights, w_gate, w_up, w_down):
    group_count = lax.axis_size("grp")
    lanes = lax.axis_size("ep")
    devices = group_count * lanes
    rows, width = tokens.shape
    order = ring_order(group_count // 2, lanes)
    chips = len(order)
    far = chips // 2
    extra = -(-devices // 16) * 16

    def device(place, core):
        x, z = order[place % chips]
        return (2 * x + core) * lanes + z

    ahead = [(device(p, c), device(p + 1, c)) for p in range(chips) for c in range(2)]
    behind = [(device(p, c), device(p - 1, c)) for p in range(chips) for c in range(2)]
    across = [(device(p, c), device(p, 1 - c)) for p in range(chips) for c in range(2)]

    def send(array, pairs):
        return lax.ppermute(array, BOTH, pairs)

    me = lax.axis_index("grp") * lanes + lax.axis_index("ep")
    other = jnp.where(lax.rem(lax.axis_index("grp"), 2) == 0, me + lanes, me - lanes)
    places = jnp.stack([me, other]).reshape(1, 2)

    cotangent = with_lines(expert_ids, route_weights, cotangent)
    grad_up, grad_down = send(cotangent, ahead), send(cotangent, behind)
    mine = (w_gate[0], w_up[0], w_down[0])
    other = tuple(send(w, across) for w in mine)
    second = after_all(tokens, *other[:2])[0]
    token_up, token_down = send(second, ahead), send(second, behind)
    weights = hold(*mine, *other)

    sums = {}

    def compute(blocks):
        kinds = []
        for o, *unused in blocks:
            left = jnp.bfloat16 if o in (far, far - 1) else jnp.float32
            right = jnp.bfloat16 if o in (far, chips - far + 1) else jnp.float32
            kinds.append((left, right))
        out = block_grads(places, [(t, g) for o, t, g in blocks], weights, extra, kinds)
        for (o, *unused), pair in zip(blocks, out):
            sums[o] = pair
        return out[0][0]

    arrived = [[(0, tokens, cotangent)], [(1, token_up, grad_up), (chips - 1, token_down, grad_down)]]
    for step in range(2, far):
        if step == far - 1:
            grad_up, grad_down = after_all(grad_up, grad_down, compute(arrived[0]))[:2]
        token_up, token_down = send(token_up, ahead), send(token_down, behind)
        grad_up, grad_down = send(grad_up, ahead), send(grad_down, behind)
        arrived.append([(step, token_up, grad_up), (chips - step, token_down, grad_down)])
    grad_down = after_all(grad_down, grad_up, *[compute(arrived[o]) for o in range(1, far - 2)])[0]
    token_up = after_all(token_up, compute(arrived[far - 2]))[0]
    token_up, grad_down = send(token_up, ahead), send(grad_down, behind)
    last = compute(arrived[far - 1])

    right_up, left_down = send(sums[chips - far + 1][1], ahead), send(sums[far - 1][0], behind)
    token_up = after_all(token_up, last)[0]
    compute([(far, token_up, grad_down)])
    left_up, right_down = after_all(*sums[far], right_up, left_down)[:2]
    for step in range(far, 0, -1):
        left_up, right_down = send(left_up, ahead), send(right_down, behind)
        if step > 2:
            right_up, left_down = add_pairs((right_up, sums[chips - step + 2][1]), (left_down, sums[step - 2][0]))
            right_up, left_down = send(right_up, ahead), send(left_down, behind)
        if step > 1:
            left_up, right_down = add_pairs((left_up, sums[chips - step + 1][0]), (right_down, sums[step - 1][1]))

    grad_tokens, grad_weights = pl.pallas_call(
        finish_kernel,
        out_shape=[
            jax.ShapeDtypeStruct(tokens.shape, tokens.dtype),
            jax.ShapeDtypeStruct(expert_ids.shape[::-1], jnp.bfloat16),
        ],
        compiler_params=pltpu.CompilerParams(vmem_limit_bytes=8 << 20),
        cost_estimate=LIGHT,
    )(*sums[0], left_up, left_down, right_up, right_down, expert_ids.T)
    return (grad_tokens, grad_weights.T)


def on_device(tokens, cotangent, expert_ids, route_weights, w_gate, w_up, w_down):
    group_count = lax.axis_size("grp")
    experts = group_count * lax.axis_size("ep")
    rows, top_count = expert_ids.shape
    capacity = 2 * rows * top_count // experts
    width = tokens.shape[1]
    fits = rows % 128 == 0 and width % (2 * rows) == 0 and experts <= rows
    fits = fits and experts >= 8 and experts % LINES == 0 and experts <= LINES * (width // rows // 3)
    fits = fits and group_count % 2 == 0 and 2 * capacity >= rows
    plan = ring_plan if fits else routed_plan
    return plan(tokens, cotangent, expert_ids, route_weights, w_gate, w_up, w_down)


def solution(mesh):
    in_specs = (
        P(("parts", "grp", "ep"), None),
        P(("parts", "grp", "ep"), None),
        P(("parts", "grp", "ep"), None),
        P(("parts", "grp", "ep"), None),
        P(("grp", "ep"), None, None),
        P(("grp", "ep"), None, None),
        P(("grp", "ep"), None, None),
    )
    out_specs = (P(("parts", "grp", "ep"), None), P(("parts", "grp", "ep"), None))
    return jax.shard_map(
        on_device, mesh=mesh, in_specs=in_specs, out_specs=out_specs, check_vma=False
    )
```
